256 devices in a mesh: replica: 16 (over y, z_hi, core), shard: 16 (over z_lo, x).
Axes of the slice: x: 4, y: 4, z: 8 (z_hi: 2, z_lo: 4; z = z_hi * 4 + z_lo), core: 2. Of those that a mesh axis runs over, the one named last changes fastest.
Arguments:
- pseudo_in: float32 [16, 2, 4096, 1536], P('replica', None, 'shard'), may hold values from -6 to 6
- pseudo_out: float32 [16, 2, 768, 4096], P('replica', None, 'shard'), may hold values from -6 to 6
- master_in: float32 [2, 4096, 1536], P(None, 'shard', 'replica'), may hold values from -6 to 6
- master_out: float32 [2, 768, 4096], P(None, 'shard', 'replica'), may hold values from -6 to 6
- moment_in: float32 [2, 4096, 1536], P(None, 'shard', 'replica'), may hold values from -4 to 4
- moment_out: float32 [2, 768, 4096], P(None, 'shard', 'replica'), may hold values from -4 to 4
- tokens: bfloat16 [16, 16, 256, 4096], P('replica', 'shard'), may hold values from -6 to 6
- route_ids: int32 [16, 16, 256, 2], P('replica', 'shard'), may hold values from 0 to 1, all different within a row
- route_weights: float32 [16, 16, 256, 2], P('replica', 'shard'), may hold values from 0.1 to 1
- counts: int32 [16, 16], P('replica', 'shard'), may hold values from 64 to 256, as said below
Outputs:
- new_master_in: float32 [2, 4096, 1536], P(None, 'shard', 'replica')
- new_master_out: float32 [2, 768, 4096], P(None, 'shard', 'replica')
- new_moment_in: float32 [2, 4096, 1536], P(None, 'shard', 'replica')
- new_moment_out: float32 [2, 768, 4096], P(None, 'shard', 'replica')
- mixed: bfloat16 [16, 16, 256, 4096], P('replica', 'shard')
The draws below stay inside these ranges and needn't reach their ends.
Inputs may be any that keep to these rules, and one draw needn't show every extreme that they name: `counts`: at least one device has all 256 row slots valid. `route_ids`: each row names both experts, one in each column.
All inputs are finite; a program needn't handle non-finite values.
Results may differ from the reference program's by a relative error of at most 0.0076.
Values may be sent and summed in bfloat16 or wider, within the bound.
No kernel may reach another device: no remote copies, remote signals or barrier semaphores. Data moves between devices by JAX's collectives and lax.ppermute only.
A program may use at most 128 MiB of HBM per device.

```python
import math
import jax
import jax.numpy as jnp
from jax import lax

D = 4096
F = 768
EXPERTS = 2
ROWS = 256
REPLICAS = 16
SHARDS = 16


def draw_counts(key, part):
    key = jax.random.fold_in(key, 11)
    first_key, second_key = jax.random.split(key)
    values = jax.random.randint(first_key, (REPLICAS * SHARDS,), ROWS // 4, ROWS + 1)
    full_spot = jax.random.randint(second_key, (), 0, REPLICAS * SHARDS)
    places = jnp.arange(REPLICAS * SHARDS, dtype=jnp.int32)
    values = jnp.where(places == full_spot, ROWS, values)
    return values.reshape(REPLICAS, SHARDS).astype(jnp.int32)


def strengthened(array, own_key, source, target, parts, factor):
    owner, partner = [(jnp.arange(array.shape[position]) // (array.shape[position] // parts)).reshape([-1 if axis == position else 1 for axis in range(array.ndim)]) for position in (source, target)]
    chosen = jax.random.permutation(own_key, parts)[partner]
    strong = (owner == chosen) | (owner == (partner + parts // 2) % parts)
    return jnp.where(strong, factor * array, array)


def shard_levels(own_key, dims, shards, low, top_value):
    def one(axis_at, shards_of):
        heights = jax.random.uniform(jax.random.fold_in(jax.random.fold_in(own_key, 6), axis_at), (shards_of,), jnp.float32, low / len(shards), top_value / len(shards))
        return jnp.repeat(jnp.exp(heights), dims[axis_at] // shards_of).reshape((-1,) + (1,) * (len(dims) - axis_at - 1))

    factor_of = one(*shards[0])
    for cut in shards[1:]:
        factor_of = factor_of * one(*cut)
    return factor_of


def choose_distinct(rng, rows, amount, top, lift):
    order = jax.random.permutation(jax.random.fold_in(rng, 1), amount)
    boost = order
    for power in range(3):
        boost = boost * boost // amount
    boost = boost * lift // amount
    lots = jax.random.randint(jax.random.fold_in(rng, 2), (rows, amount), 0, 4096) + boost
    holders = jax.random.permutation(jax.random.fold_in(rng, 3), rows)[jnp.arange(amount) % rows]
    lots = jnp.where(jnp.arange(rows)[:, None] == holders[None, :], 1 << 14, lots)
    priority = lots * amount + jnp.arange(amount)
    return lax.top_k(priority.astype(jnp.int32), top)[1].astype(jnp.int32)


def gaussian(rng, dims, scale, reach, pieces=(), kind=jnp.bfloat16):
    loudness = shard_levels(rng, dims, pieces, -0.22, 0.18) if pieces else 1.0
    entries = jax.random.normal(rng, dims, jnp.float32) * scale * loudness
    return jnp.minimum(jnp.maximum(entries, -reach), reach).astype(kind)


def heavy_noise(own_key, shape, width, bound, cuts, heavy, kind=jnp.bfloat16):
    entries = width * jax.random.normal(own_key, shape, jnp.float32)
    if cuts:
        entries = entries * shard_levels(own_key, shape, cuts, -0.22, 0.18)
    return jnp.clip(strengthened(entries, jax.random.fold_in(own_key, 3), *heavy), -bound, bound).astype(kind)


def setup_inputs(seed: int = 0) -> dict:
    key_list = jax.random.split(jax.random.key(seed), 11)
    pseudo_in = heavy_noise(key_list[0], (REPLICAS, EXPERTS, D, 2 * F), 1.0, 6.0, ((0, 16), (2, 16)), (0, 3, 16, 2.0), jnp.float32)
    pseudo_out = heavy_noise(key_list[1], (REPLICAS, EXPERTS, F, D), 1.0, 6.0, ((0, 16), (2, 16)), (0, 3, 16, 2.0), jnp.float32)
    master_in = gaussian(key_list[2], (EXPERTS, D, 2 * F), 1.0, 6.0, ((1, 16), (2, 16)), jnp.float32)
    master_out = gaussian(key_list[3], (EXPERTS, F, D), 1.0, 6.0, ((1, 16), (2, 16)), jnp.float32)
    moment_in = gaussian(key_list[4], (EXPERTS, D, 2 * F), 0.5, 4.0, ((1, 16), (2, 16)), jnp.float32)
    moment_out = gaussian(key_list[5], (EXPERTS, F, D), 0.5, 4.0, ((1, 16), (2, 16)), jnp.float32)
    tokens = gaussian(key_list[6], (REPLICAS, SHARDS, ROWS, D), 1.0, 6.0, ((0, 16), (1, 16)))
    route_ids = choose_distinct(key_list[7], REPLICAS * SHARDS * ROWS, EXPERTS, 2, 0).reshape((REPLICAS, SHARDS, ROWS, 2))
    route_weights = jnp.clip(0.1 + 0.9 * jax.random.uniform(key_list[8], (REPLICAS, SHARDS, ROWS, 2), jnp.float32) ** shard_levels(key_list[8], (REPLICAS, SHARDS, ROWS, 2), ((0, 16), (1, 16)), -0.2, 0.2), 0.1, 1.0)
    counts = draw_counts(jax.random.fold_in(key_list[10], 71), 0)
    return {"pseudo_in": pseudo_in, "pseudo_out": pseudo_out, "master_in": master_in, "master_out": master_out, "moment_in": moment_in, "moment_out": moment_out, "tokens": tokens, "route_ids": route_ids, "route_weights": route_weights, "counts": counts}


outer_rate = 0.7
outer_momentum = 0.9

def outer_update(pseudo, master, moment):
    delta = lax.optimization_barrier(jnp.sum(pseudo, axis=0)) / REPLICAS
    moment_new = outer_momentum * moment + delta
    master_new = master - outer_rate * (delta + outer_momentum * moment_new)
    return (master_new, moment_new)

def rounded(values):
    low = lax.optimization_barrier(values.astype(jnp.bfloat16))
    return low.astype(jnp.float32)

def reference(pseudo_in, pseudo_out, master_in, master_out, moment_in, moment_out, tokens, route_ids, route_weights, counts):
    new_master_in, new_moment_in = outer_update(pseudo_in, master_in, moment_in)
    new_master_out, new_moment_out = outer_update(pseudo_out, master_out, moment_out)
    weights_in = rounded(new_master_in)
    weights_out = rounded(new_master_out)
    scale_in = 1.0 / math.sqrt(D)
    scale_out = 1.0 / math.sqrt(F)

    def one_replica(blocks):
        token_rows, expert_ids, gate_gains, row_count = blocks
        flat_rows = token_rows.reshape(SHARDS * ROWS, D).astype(jnp.float32)
        combined = jnp.zeros((SHARDS * ROWS, D), jnp.float32)
        for expert in range(EXPERTS):
            projected = jnp.dot(flat_rows, weights_in[expert], precision=lax.Precision.HIGHEST) * scale_in
            hidden = rounded(jax.nn.silu(projected[:, :F]) * projected[:, F:])
            expert_out = rounded(jnp.dot(hidden, weights_out[expert], precision=lax.Precision.HIGHEST) * scale_out)
            gate_gain = lax.optimization_barrier(jnp.sum(gate_gains * (expert_ids == expert).astype(jnp.float32), axis=-1)).reshape(-1)
            combined = combined + gate_gain[:, None] * expert_out
        valid_rows = (jnp.arange(ROWS, dtype=jnp.int32)[None, :] < row_count[:, None]).astype(jnp.float32).reshape(-1)
        return (valid_rows[:, None] * combined).astype(jnp.bfloat16).reshape(SHARDS, ROWS, D)
    mixed = lax.map(one_replica, (tokens, route_ids, route_weights, counts))
    return (new_master_in, new_master_out, new_moment_in, new_moment_out, mixed)
```

```python
import itertools
import math

import jax
import jax.numpy as jnp
from jax import lax
from jax.experimental import pallas as pl
from jax.experimental.pallas import tpu as pltpu
from jax.sharding import Mesh
from jax.sharding import PartitionSpec as P

D = 4096
F = 768
REPLICAS = 16

outer_rate = 0.7
outer_momentum = 0.9

AXES = ("y", "zh", "core", "zl", "x")
SIZES = (4, 2, 2, 4, 4)
PLACES = list(itertools.product(*(range(n) for n in SIZES)))
NUMBER = {place: i for i, place in enumerate(PLACES)}
LENGTH = {"x": 4, "y": 4, "z": 8}
bf16 = jnp.bfloat16
f32 = jnp.float32


def moved(block, axis, step):
    route = []
    for y, zh, core, zl, x in PLACES:
        z = zh * 4 + zl
        if axis == "x":
            x2, y2, z2 = (x + step) % 4, y, z
        elif axis == "y":
            x2, y2, z2 = x, (y + step) % 4, z
        else:
            x2, y2, z2 = x, y, (z + step) % 8
        route.append((NUMBER[(y, zh, core, zl, x)], NUMBER[(y2, z2 // 4, core, z2 % 4, x2)]))
    return lax.ppermute(block, AXES, route)


def core_swap(block):
    return lax.ppermute(block, "core", [(0, 1), (1, 0)])


def pick(array, index):
    return lax.dynamic_index_in_dim(array, index, 0, keepdims=False)


def together(*arrays):
    return lax.optimization_barrier(tuple(arrays))


def place(blocks, indices, parts, out_shapes):
    count = len(blocks)

    def kernel(index_ref, *refs):
        ins, outs = refs[:count], refs[count:]
        for j in range(count):
            at = index_ref[j]
            for o, source, target in parts[j]:
                outs[o][target(at)] = ins[j][source]

    vmem = pl.BlockSpec(memory_space=pltpu.VMEM)
    return pl.pallas_call(
        kernel,
        in_specs=[pl.BlockSpec(memory_space=pltpu.SMEM)] + [vmem] * count,
        out_specs=[vmem] * len(out_shapes),
        out_shape=[jax.ShapeDtypeStruct(s, bf16) for s in out_shapes],
    )(jnp.stack(indices).astype(jnp.int32), *blocks)


def span(start, size, unit):
    return pl.ds(pl.multiple_of(start, unit), size)


EVERY = slice(None)


def place_z(blocks, indices):
    parts = [
        [
            (
                o,
                (EVERY, slice(o * 128, o * 128 + 128)),
                lambda at: (span((at // 4) * 192, 192, 32), span((at % 4) * 128, 128, 128)),
            )
            for o in range(2)
        ]
    ] * 8
    return place(blocks, indices, parts, [(384, 512), (384, 512)])


def around(index):
    return [index, (index + 3) % 4, (index + 1) % 4, (index + 2) % 4]


def place_middle(rows_blocks, columns_blocks, y, x):
    parts = [[(0, (EVERY, EVERY), lambda at: (span(at * 384, 384, 32), EVERY))]] * 4
    parts += [[(1, (EVERY, EVERY), lambda at: (EVERY, span(at * 512, 512, 128)))]] * 4
    return place(
        [*rows_blocks, *columns_blocks], around(y) + around(x), parts, [(1536, 512), (384, 2048)]
    )


def order_tokens(own, other):
    def kernel(own_ref, other_ref, first_ref, second_ref):
        for k, ref in enumerate((own_ref, other_ref)):
            rows = slice(k * 256, k * 256 + 256)
            for zl in range(4):
                for x in range(4):
                    start = (zl * 4 + x) * 256
                    to = zl * 128
                    first_ref[x, rows, to : to + 128] = ref[:, start : start + 128]
                    to += x * 512
                    second_ref[rows, to : to + 128] = ref[:, start + 128 : start + 256]

    vmem = pl.BlockSpec(memory_space=pltpu.VMEM)
    return pl.pallas_call(
        kernel,
        in_specs=[vmem] * 2,
        out_specs=[vmem] * 2,
        out_shape=[jax.ShapeDtypeStruct((4, 512, 512), bf16), jax.ShapeDtypeStruct((512, 2048), bf16)],
        compiler_params=pltpu.CompilerParams(vmem_limit_bytes=32 * 2**20),
    )(own, other)


def swiglu(y, gates, ups, by_step):
    scale = 1.0 / math.sqrt(D)

    def kernel(y_ref, gates_ref, ups_ref, *refs):
        blocks, out_ref = refs[:4], refs[4]

        def write(here):
            for k in range(2):
                cut = slice(k * 384, k * 384 + 384)
                gate = (gates_ref[:, cut] + blocks[(k - here) % 4][...]) * scale
                up = (ups_ref[:, cut] + blocks[(k + 2 - here) % 4][...]) * scale
                out_ref[:, cut] = (jax.nn.silu(gate) * up).astype(bf16)

        for here in range(4):
            pl.when(y_ref[0] == here)(lambda here=here: write(here))

    vmem = pl.BlockSpec(memory_space=pltpu.VMEM)
    return pl.pallas_call(
        kernel,
        in_specs=[pl.BlockSpec(memory_space=pltpu.SMEM)] + [vmem] * 6,
        out_specs=vmem,
        out_shape=jax.ShapeDtypeStruct((512, F), bf16),
        compiler_params=pltpu.CompilerParams(vmem_limit_bytes=32 * 2**20),
    )(y.astype(jnp.int32).reshape(1), gates, ups, *by_step)


def outer_update(delta, master, moment):
    moment_new = outer_momentum * moment + delta
    master_new = master - outer_rate * (delta + outer_momentum * moment_new)
    return master_new, moment_new


def combine(own, back, gain_own, gain_other):
    def kernel(own_0, own_1, back_0, back_1, gain_own_ref, gain_other_ref, out_ref):
        for zh, (a, b) in enumerate(((own_0, back_0), (own_1, back_1))):
            out_ref[:, zh * 512 : zh * 512 + 512] = (
                gain_own_ref[...] * a[...].astype(f32) + gain_other_ref[...] * b[...].astype(f32)
            ).astype(bf16)

    block = pl.BlockSpec((256, 512), lambda i: (0, i))
    gain = pl.BlockSpec((256, 1), lambda i: (0, 0))
    return pl.pallas_call(
        kernel,
        grid=(4,),
        in_specs=[block] * 4 + [gain] * 2,
        out_specs=pl.BlockSpec((256, 1024), lambda i: (0, i)),
        out_shape=jax.ShapeDtypeStruct((256, 4096), bf16),
    )(*own, *back, gain_own, gain_other)


def nt_dot(rows, columns):
    return lax.dot_general(rows, columns, (((1,), (1,)), ((), ())), preferred_element_type=f32)


def body(
    pseudo_in,
    pseudo_out,
    master_in,
    master_out,
    moment_in,
    moment_out,
    tokens,
    route_ids,
    route_weights,
    counts,
):
    core = lax.axis_index("core")
    x = lax.axis_index("x")
    y = lax.axis_index("y")
    zh = lax.axis_index("zh")
    z = zh * 4 + lax.axis_index("zl")
    first_core = core == 0

    own_rows = tokens[0, 0]

    def rows_of(a_in, a_out):
        return jnp.concatenate([a_in.transpose(0, 2, 1), a_out], axis=1)

    states = jnp.stack([rows_of(master_in, master_out), rows_of(moment_in, moment_out)], axis=1)

    grads_in = pseudo_in[0].astype(bf16).transpose(0, 2, 1).reshape(2, 8, 192, 256)
    grads_out = (
        pseudo_out[0].astype(bf16).reshape(2, 48, 8, 2, 256).transpose(0, 2, 3, 1, 4).reshape(2, 8, 96, 256)
    )
    other_in, other_out = together(pick(grads_in, 1 - core), pick(grads_out, 1 - core))
    got_in, got_out = together(core_swap(other_in), core_swap(other_out))
    sum_in = (pick(grads_in, core).astype(f32) + got_in.astype(f32)).reshape(4, 2, 192, 256)
    sum_out = (pick(grads_out, core).astype(f32) + got_out.astype(f32)).reshape(4, 2, 96, 256)

    def to_y(total):
        low = total.astype(bf16)
        return [pick(low, (y + k) % 4) for k in (1, 3, 2)]

    def over_y(sends):
        return [moved(s, "y", k) for s, k in zip(sends, (1, 3, 2))]

    def add_y(total, got):
        kept = pick(total, y)
        for g in got:
            kept = kept + g.astype(f32)
        return pick(kept, zh), pick(kept, 1 - zh).astype(bf16)

    *s_in, token_rows, states = together(*to_y(sum_in), own_rows, states)
    *got, other_rows, state_got = together(
        *over_y(s_in), core_swap(token_rows), core_swap(pick(states, 1 - core))
    )
    keep_in, send_in = add_y(sum_in, got)
    s_out = to_y(sum_out)
    state_own = pick(states, core)
    send_in, state_own, state_got, *s_out = together(send_in, state_own, state_got, *s_out)
    state = jnp.where(
        first_core, jnp.stack([state_own, state_got], 1), jnp.stack([state_got, state_own], 1)
    )
    got_in, state, *got = together(moved(send_in, "z", 4), state, *over_y(s_out))

    delta_in = (keep_in + got_in.astype(f32)) / REPLICAS
    new_master_a, new_moment_a = outer_update(
        delta_in.reshape(2, 96, 256), state[0, :, :96], state[1, :, :96]
    )
    keep_out, send_out = add_y(sum_out, got)

    w_in = new_master_a.astype(bf16).reshape(192, 256)
    w_in, send_out, token_rows, other_rows = together(w_in, send_out, token_rows, other_rows)
    rows_0, rows_1 = order_tokens(token_rows, other_rows)
    b_1, f_1, f_4, got_out, rows_0, rows_1 = together(
        moved(w_in, "z", 1),
        moved(w_in, "z", -1),
        moved(w_in, "z", 4),
        moved(send_out, "z", 4),
        rows_0,
        rows_1,
    )
    delta_out = (keep_out + got_out.astype(f32)) / REPLICAS
    new_master_b, new_moment_b = outer_update(
        delta_out.reshape(2, 48, 256), state[0, :, 96:], state[1, :, 96:]
    )
    w_out = new_master_b.astype(bf16).reshape(96, 256)
    b_1, f_1, f_4, w_out = together(b_1, f_1, f_4, w_out)
    b_2, f_3, f_2, b_3, *o = together(
        moved(b_1, "z", 1),
        moved(f_4, "z", 1),
        moved(f_1, "z", -1),
        moved(f_4, "z", -1),
        *[moved(w_out, "y", k) for k in (1, -1, 2)],
    )
    parts = [
        [
            (0, (slice(c * 48, c * 48 + 48), EVERY), lambda at, c=c: (EVERY, span(at * 512 + c * 256, 256, 128)))
            for c in range(2)
        ]
    ] * 4
    p2 = place([w_out, *o], around(y), parts, [(48, 2048)])[0]
    o = [moved(p2, "x", k) for k in (1, -1, 2)]
    parts = [[(0, (EVERY, EVERY), lambda at: (span(at * 48, 48, 16), EVERY))]] * 4
    p2 = place([p2, *o], around(x), parts, [(192, 2048)])[0]
    weights_out = lax.all_gather(p2, ("zh", "zl"), tiled=True).reshape(2, 768, 2048)
    p0, p1 = place_z(
        [w_in, b_1, b_2, b_3, f_1, f_2, f_3, f_4], [(z + k) % 8 for k in (0, 7, 6, 5, 1, 2, 3, 4)]
    )

    p0, p1 = together(p0, p1)
    o = together(*[moved(p0, "y", k) for k in (1, -1, 2)], *[moved(p1, "x", k) for k in (1, -1, 2)])
    p0, p1 = place_middle([p0, *o[:3]], [p1, *o[3:]], y, x)
    updated = jnp.stack(
        [
            jnp.concatenate([new_master_a, new_master_b], axis=1),
            jnp.concatenate([new_moment_a, new_moment_b], axis=1),
        ],
        axis=1,
    )
    p0, p1, updated = together(p0, p1, updated)

    def rows_x(step):
        return pick(rows_0, (x + step) % 4)

    mine = pick(updated, core)
    a_l, a_r, b_l, b_r, mine, got, total, here = together(
        moved(p0, "x", 1),
        moved(p0, "x", -1),
        moved(p1, "y", 1),
        moved(p1, "y", -1),
        mine,
        core_swap(pick(updated, 1 - core)),
        nt_dot(rows_x(0), p0),
        nt_dot(rows_1, p1),
    )
    final = jnp.where(first_core, jnp.stack([mine, got], 1), jnp.stack([got, mine], 1))
    new_in, new_out = final[:, :, :96].transpose(0, 1, 3, 2), final[:, :, 96:]
    cuts = a_l[:768], a_r[768:], b_l[:192], b_r[192:]
    total = total + nt_dot(rows_x(3), a_l) + nt_dot(rows_x(1), a_r)
    before, after = nt_dot(rows_1, b_l), nt_dot(rows_1, b_r)
    a_3, a_4, b_3, b_4, total, before, after, new_in, new_out = together(
        moved(cuts[0], "x", 1),
        moved(cuts[1], "x", -1),
        moved(cuts[2], "y", 1),
        moved(cuts[3], "y", -1),
        total,
        before,
        after,
        new_in,
        new_out,
    )
    opposite = rows_x(2)
    gates = total[:, :F] + nt_dot(opposite, a_3)
    ups = total[:, F:] + nt_dot(opposite, a_4)
    across = jnp.concatenate([nt_dot(rows_1, b_3), nt_dot(rows_1, b_4)], axis=1)
    hidden = swiglu(y, gates, ups, [here, after, across, before])

    scale_out = 1.0 / math.sqrt(F)

    def expert(part):
        return [
            (jnp.dot(part, weights_out[k], preferred_element_type=f32) * scale_out).astype(bf16)
            for k in range(2)
        ]

    back = [core_swap(o) for o in expert(hidden[256:])]
    out_own = expert(hidden[:256])

    expert_ids = route_ids[0, 0]
    gate_gains = route_weights[0, 0]
    valid_rows = (jnp.arange(256, dtype=jnp.int32) < counts[0, 0]).astype(f32)
    gain_own = valid_rows * jnp.sum(gate_gains * (expert_ids == core).astype(f32), axis=1)
    gain_other = valid_rows * jnp.sum(gate_gains * (expert_ids != core).astype(f32), axis=1)
    mixed = combine(out_own, back, gain_own[:, None], gain_other[:, None])

    return new_in[0], new_out[0], new_in[1], new_out[1], mixed[None, None]


def solution(mesh):
    fine = Mesh(mesh.devices.reshape(SIZES), AXES)
    replica, shard = ("y", "zh", "core"), ("zl", "x")
    state = P(None, shard, replica)
    in_specs = (
        P(replica, None, shard, None),
        P(replica, None, shard, None),
        state,
        state,
        state,
        state,
        P(replica, shard, None, None),
        P(replica, shard, None, None),
        P(replica, shard, None, None),
        P(replica, shard),
    )
    out_specs = (state, state, state, state, P(replica, shard, None, None))
    return jax.shard_map(body, mesh=fine, in_specs=in_specs, out_specs=out_specs, check_vma=False)
```

```python
import itertools
import math

import jax
import jax.numpy as jnp
from jax import lax
from jax.experimental import pallas as pl
from jax.experimental.pallas import tpu as pltpu
from jax.sharding import Mesh
from jax.sharding import PartitionSpec as P

D = 4096
F = 768
REPLICAS = 16

outer_rate = 0.7
outer_momentum = 0.9

AXES = ("y", "zh", "core", "zl", "x")
SIZES = (4, 2, 2, 4, 4)
PLACES = list(itertools.product(*(range(n) for n in SIZES)))
NUMBER = {place: i for i, place in enumerate(PLACES)}
LENGTH = {"x": 4, "y": 4, "z": 8}
bf16 = jnp.bfloat16
f32 = jnp.float32


def moved(block, axis, step):
    route = []
    for y, zh, core, zl, x in PLACES:
        z = zh * 4 + zl
        if axis == "x":
            x2, y2, z2 = (x + step) % 4, y, z
        elif axis == "y":
            x2, y2, z2 = x, (y + step) % 4, z
        else:
            x2, y2, z2 = x, y, (z + step) % 8
        route.append((NUMBER[(y, zh, core, zl, x)], NUMBER[(y2, z2 // 4, core, z2 % 4, x2)]))
    return lax.ppermute(block, AXES, route)


def core_swap(block):
    return lax.ppermute(block, "core", [(0, 1), (1, 0)])


def pick(array, index):
    return lax.dynamic_index_in_dim(array, index, 0, keepdims=False)


def together(*arrays):
    return lax.optimization_barrier(tuple(arrays))


def place(blocks, index, offset, parts, out_shapes):
    count = len(blocks)

    def kernel(index_ref, *refs):
        ins, outs = refs[:count], refs[count:]
        for j in range(count):
            at = index_ref[offset + j]
            for o, source, target in parts[j]:
                outs[o][target(at)] = ins[j][source]

    vmem = pl.BlockSpec(memory_space=pltpu.VMEM)
    return pl.pallas_call(
        kernel,
        in_specs=[pl.BlockSpec(memory_space=pltpu.SMEM)] + [vmem] * count,
        out_specs=[vmem] * len(out_shapes),
        out_shape=[jax.ShapeDtypeStruct(s, bf16) for s in out_shapes],
        compiler_params=pltpu.CompilerParams(vmem_limit_bytes=32 * 2**20),
    )(index, *blocks)


def span(start, size, unit):
    return pl.ds(pl.multiple_of(start, unit), size)


EVERY = slice(None)


def place_z(blocks, index):
    parts = [
        [
            (
                o,
                (EVERY, slice(o * 128, o * 128 + 128)),
                lambda at: (span((at // 4) * 192, 192, 32), span((at % 4) * 128, 128, 128)),
            )
            for o in range(2)
        ]
    ] * 8
    return place(blocks, index, 0, parts, [(384, 512), (384, 512)])


def around(index):
    return [index, (index + 3) % 4, (index + 1) % 4, (index + 2) % 4]


def place_middle(rows_blocks, columns_blocks, index):
    halves = [(EVERY, slice(0, 256)), (EVERY, slice(256, 512))]
    parts = [
        [(o, halves[o], lambda at: (span(at * 384, 384, 32), EVERY)) for o in range(2)]
    ] * 4
    parts += [
        [(2 + o, halves[o], lambda at: (EVERY, span(at * 256, 256, 128))) for o in range(2)]
    ] * 4
    return place(
        [*rows_blocks, *columns_blocks], index, 8, parts, [(1536, 256)] * 2 + [(384, 1024)] * 2
    )


def order_tokens(own, other):
    def kernel(own_ref, other_ref, *outs):
        for k, ref in enumerate((own_ref, other_ref)):
            rows = slice(k * 256, k * 256 + 256)
            for zl in range(4):
                for x in range(4):
                    start = (zl * 4 + x) * 256
                    to = zl % 2 * 128
                    outs[zl // 2][x, rows, to : to + 128] = ref[:, start : start + 128]
                    to += x * 256
                    outs[2 + zl // 2][rows, to : to + 128] = ref[:, start + 128 : start + 256]

    vmem = pl.BlockSpec(memory_space=pltpu.VMEM)
    return pl.pallas_call(
        kernel,
        in_specs=[vmem] * 2,
        out_specs=[vmem] * 4,
        out_shape=[jax.ShapeDtypeStruct(s, bf16) for s in [(4, 512, 256)] * 2 + [(512, 1024)] * 2],
        compiler_params=pltpu.CompilerParams(vmem_limit_bytes=32 * 2**20),
    )(own, other)


def swiglu(y, total, by_step):
    scale = 1.0 / math.sqrt(D)

    def kernel(y_ref, total_ref, *refs):
        blocks, out_ref = refs[:4], refs[4]

        def write(here):
            for k in range(2):
                cut = slice(k * 384, k * 384 + 384)
                up_cut = slice(F + k * 384, F + k * 384 + 384)
                gate = (total_ref[:, cut] + blocks[(k - here) % 4][...]) * scale
                up = (total_ref[:, up_cut] + blocks[(k + 2 - here) % 4][...]) * scale
                out_ref[:, cut] = (jax.nn.silu(gate) * up).astype(bf16)

        for here in range(4):
            pl.when(y_ref[0] == here)(lambda here=here: write(here))

    vmem = pl.BlockSpec(memory_space=pltpu.VMEM)
    return pl.pallas_call(
        kernel,
        in_specs=[pl.BlockSpec(memory_space=pltpu.SMEM)] + [vmem] * 5,
        out_specs=vmem,
        out_shape=jax.ShapeDtypeStruct((512, F), bf16),
        compiler_params=pltpu.CompilerParams(vmem_limit_bytes=32 * 2**20),
    )(y.astype(jnp.int32).reshape(1), total, *by_step)


def outer_update(delta, master, moment):
    moment_new = outer_momentum * moment + delta
    master_new = master - outer_rate * (delta + outer_momentum * moment_new)
    return master_new, moment_new


def combine(own, back, gain_own, gain_other):
    def kernel(own_0, own_1, back_0, back_1, gain_own_ref, gain_other_ref, out_ref):
        for zh, (a, b) in enumerate(((own_0, back_0), (own_1, back_1))):
            out_ref[:, zh * 512 : zh * 512 + 512] = (
                gain_own_ref[...] * a[...].astype(f32) + gain_other_ref[...] * b[...].astype(f32)
            ).astype(bf16)

    block = pl.BlockSpec((256, 512), lambda i: (0, i))
    gain = pl.BlockSpec((256, 1), lambda i: (0, 0))
    return pl.pallas_call(
        kernel,
        grid=(4,),
        in_specs=[block] * 4 + [gain] * 2,
        out_specs=pl.BlockSpec((256, 1024), lambda i: (0, i)),
        out_shape=jax.ShapeDtypeStruct((256, 4096), bf16),
    )(*own, *back, gain_own, gain_other)


def nt_dot(rows, columns):
    return lax.dot_general(rows, columns, (((1,), (1,)), ((), ())), preferred_element_type=f32)


def body(
    pseudo_in,
    pseudo_out,
    master_in,
    master_out,
    moment_in,
    moment_out,
    tokens,
    route_ids,
    route_weights,
    counts,
):
    core = lax.axis_index("core")
    x = lax.axis_index("x")
    y = lax.axis_index("y")
    zh = lax.axis_index("zh")
    z = zh * 4 + lax.axis_index("zl")
    first_core = core == 0

    own_rows = tokens[0, 0]

    def rows_of(a_in, a_out):
        return jnp.concatenate([a_in.transpose(0, 2, 1), a_out], axis=1)

    states = jnp.stack([rows_of(master_in, master_out), rows_of(moment_in, moment_out)], axis=1)

    grads_in = pseudo_in[0].astype(bf16).transpose(0, 2, 1).reshape(2, 8, 192, 256)
    grads_out = (
        pseudo_out[0].astype(bf16).reshape(2, 48, 8, 2, 256).transpose(0, 2, 3, 1, 4).reshape(2, 8, 96, 256)
    )
    grads = jnp.concatenate([grads_in, grads_out], axis=2)
    got = core_swap(pick(grads, 1 - core))
    total = (pick(grads, core).astype(f32) + got.astype(f32)).reshape(4, 2, 288, 256)
    low = total.astype(bf16)
    index = jnp.stack(
        [(z + k) % 8 for k in (0, 7, 6, 5, 1, 2, 3, 4)] + around(y) + around(x)
    ).astype(jnp.int32)
    *sends, kept, token_rows, states, index = together(
        *[pick(low, (y + k) % 4) for k in (1, 3, 2)], pick(total, y), own_rows, states, index
    )
    *got, other_rows, state_got, index = together(
        *[moved(s, "y", k) for s, k in zip(sends, (1, 3, 2))],
        core_swap(token_rows),
        core_swap(pick(states, 1 - core)),
        index,
    )
    for g in got:
        kept = kept + g.astype(f32)
    state_own = pick(states, core)
    send, kept, state_own, state_got = together(
        pick(kept, 1 - zh).astype(bf16), pick(kept, zh), state_own, state_got
    )
    state = jnp.where(
        first_core, jnp.stack([state_own, state_got], 1), jnp.stack([state_got, state_own], 1)
    )
    got, state = together(moved(send, "z", 4), state)
    delta = (kept + got.astype(f32)) / REPLICAS
    new_master_a, new_moment_a = outer_update(
        delta[:192].reshape(2, 96, 256), state[0, :, :96], state[1, :, :96]
    )
    new_master_b, new_moment_b = outer_update(
        delta[192:].reshape(2, 48, 256), state[0, :, 96:], state[1, :, 96:]
    )

    w_in = new_master_a.astype(bf16).reshape(192, 256)
    w_out = new_master_b.astype(bf16).reshape(96, 256)
    w_in, w_out, token_rows, other_rows = together(w_in, w_out, token_rows, other_rows)
    rows = order_tokens(token_rows, other_rows)
    b_1, f_1, f_4, *rest = together(
        moved(w_in, "z", 1),
        moved(w_in, "z", -1),
        moved(w_in, "z", 4),
        *[moved(w_out, "y", k) for k in (1, -1, 2)],
        *rows,
    )
    o, rows = rest[:3], rest[3:]
    parts = [
        [
            (0, (slice(c * 48, c * 48 + 48), EVERY), lambda at, c=c: (EVERY, span(at * 512 + c * 256, 256, 128)))
            for c in range(2)
        ]
    ] * 4
    p2 = place([w_out, *o], index, 8, parts, [(48, 2048)])[0]
    b_1, f_1, f_4, p2 = together(b_1, f_1, f_4, p2)
    b_2, f_3, f_2, b_3, *o = together(
        moved(b_1, "z", 1),
        moved(f_4, "z", 1),
        moved(f_1, "z", -1),
        moved(f_4, "z", -1),
        *[moved(p2, "x", k) for k in (1, -1, 2)],
    )
    parts = [[(0, (EVERY, EVERY), lambda at: (span(at * 48, 48, 16), EVERY))]] * 4
    p2 = place([p2, *o], index, 12, parts, [(192, 2048)])[0]
    p0, p1 = place_z([w_in, b_1, b_2, b_3, f_1, f_2, f_3, f_4], index)
    p0, p1, p2 = together(p0, p1, p2)
    weights_out = lax.all_gather(p2, ("zh", "zl"), tiled=True)

    updated = jnp.stack(
        [
            jnp.concatenate([new_master_a, new_master_b], axis=1),
            jnp.concatenate([new_moment_a, new_moment_b], axis=1),
        ],
        axis=1,
    )
    *o, updated = together(
        *[moved(p0, "y", k) for k in (1, -1, 2)], *[moved(p1, "x", k) for k in (1, -1, 2)], updated
    )
    p = place_middle([p0, *o[:3]], [p1, *o[3:]], index)
    *p, updated = together(*p, updated)

    def x_dot(half, step, block):
        return nt_dot(pick(rows[half], (x + step) % 4), block)

    def y_dot(half, block):
        return nt_dot(rows[2 + half], block)

    mine = pick(updated, core)
    x_l, x_r, y_l, y_r, mine, got, total, here = together(
        moved(p[0], "x", 1),
        moved(p[1], "x", -1),
        moved(p[2], "y", 1),
        moved(p[3], "y", -1),
        mine,
        core_swap(pick(updated, 1 - core)),
        x_dot(0, 0, p[0]) + x_dot(1, 0, p[1]),
        y_dot(0, p[2]) + y_dot(1, p[3]),
    )
    final = jnp.where(first_core, jnp.stack([mine, got], 1), jnp.stack([got, mine], 1))
    new_in, new_out = final[:, :, :96].transpose(0, 1, 3, 2), final[:, :, 96:]
    x_l2, x_r2 = moved(p[1], "x", 1), moved(p[0], "x", -1)
    y_l2, y_r2 = moved(p[3], "y", 1), moved(p[2], "y", -1)
    x_o, x_o2 = moved(x_l, "x", 1), moved(x_r, "x", -1)
    y_o, y_o2 = moved(y_l, "y", 1), moved(y_r, "y", -1)
    (total,) = together(total + x_dot(0, 3, x_l))
    (total,) = together(total + x_dot(1, 1, x_r))
    before, after = y_dot(0, y_l), y_dot(1, y_r)
    (total,) = together(total + x_dot(1, 3, x_l2))
    (total,) = together(total + x_dot(0, 1, x_r2))
    before, after = before + y_dot(1, y_l2), after + y_dot(0, y_r2)
    x_o, x_o2, y_o, y_o2, new_in, new_out, weights_out = together(
        x_o, x_o2, y_o, y_o2, new_in, new_out, weights_out
    )
    weights_out = weights_out.reshape(2, 768, 2048)
    across = y_dot(0, y_o) + y_dot(1, y_o2)
    (total,) = together(total + x_dot(0, 2, x_o))
    total = total + x_dot(1, 2, x_o2)
    hidden = swiglu(y, total, [here, after, across, before])

    scale_out = 1.0 / math.sqrt(F)

    def expert(part):
        return [
            (jnp.dot(part, weights_out[k], preferred_element_type=f32) * scale_out).astype(bf16)
            for k in range(2)
        ]

    back = [core_swap(o) for o in expert(hidden[256:])]
    out_own = expert(hidden[:256])

    expert_ids = route_ids[0, 0]
    gate_gains = route_weights[0, 0]
    valid_rows = (jnp.arange(256, dtype=jnp.int32) < counts[0, 0]).astype(f32)
    gain_own = valid_rows * jnp.sum(gate_gains * (expert_ids == core).astype(f32), axis=1)
    gain_other = valid_rows * jnp.sum(gate_gains * (expert_ids != core).astype(f32), axis=1)
    mixed = combine(out_own, back, gain_own[:, None], gain_other[:, None])

    return new_in[0], new_out[0], new_in[1], new_out[1], mixed[None, None]


def solution(mesh):
    fine = Mesh(mesh.devices.reshape(SIZES), AXES)
    replica, shard = ("y", "zh", "core"), ("zl", "x")
    state = P(None, shard, replica)
    in_specs = (
        P(replica, None, shard, None),
        P(replica, None, shard, None),
        state,
        state,
        state,
        state,
        P(replica, shard, None, None),
        P(replica, shard, None, None),
        P(replica, shard, None, None),
        P(replica, shard),
    )
    out_specs = (state, state, state, state, P(replica, shard, None, None))
    return jax.shard_map(body, mesh=fine, in_specs=in_specs, out_specs=out_specs, check_vma=False)
```

```python
import itertools
import math

import jax
import jax.numpy as jnp
from jax import lax
from jax.experimental import pallas as pl
from jax.experimental.pallas import tpu as pltpu
from jax.sharding import Mesh
from jax.sharding import PartitionSpec as P

D = 4096
F = 768
REPLICAS = 16

outer_rate = 0.7
outer_momentum = 0.9

AXES = ("y", "zh", "core", "zl", "x")
SIZES = (4, 2, 2, 4, 4)
PLACES = list(itertools.product(*(range(n) for n in SIZES)))
NUMBER = {place: i for i, place in enumerate(PLACES)}
LENGTH = {"x": 4, "y": 4, "z": 8}
VMEM = 12 * 2**20
bf16 = jnp.bfloat16
f32 = jnp.float32


def moved(block, axis, step):
    route = []
    for y, zh, core, zl, x in PLACES:
        z = zh * 4 + zl
        if axis == "x":
            x2, y2, z2 = (x + step) % 4, y, z
        elif axis == "y":
            x2, y2, z2 = x, (y + step) % 4, z
        else:
            x2, y2, z2 = x, y, (z + step) % 8
        route.append((NUMBER[(y, zh, core, zl, x)], NUMBER[(y2, z2 // 4, core, z2 % 4, x2)]))
    return lax.ppermute(block, AXES, route)


def core_swap(block):
    return lax.ppermute(block, "core", [(0, 1), (1, 0)])


def pick(array, index):
    return lax.dynamic_index_in_dim(array, index, 0, keepdims=False)


def together(*arrays):
    return lax.optimization_barrier(tuple(arrays))


def place(blocks, index, offset, parts, out_shapes):
    count = len(blocks)

    def kernel(index_ref, *refs):
        ins, outs = refs[:count], refs[count:]
        for j in range(count):
            at = index_ref[offset + j]
            for o, source, target in parts[j]:
                outs[o][target(at)] = ins[j][source]

    vmem = pl.BlockSpec(memory_space=pltpu.VMEM)
    return pl.pallas_call(
        kernel,
        in_specs=[pl.BlockSpec(memory_space=pltpu.SMEM)] + [vmem] * count,
        out_specs=[vmem] * len(out_shapes),
        out_shape=[jax.ShapeDtypeStruct(s, bf16) for s in out_shapes],
        compiler_params=pltpu.CompilerParams(vmem_limit_bytes=VMEM),
    )(index, *blocks)


def span(start, size, unit):
    return pl.ds(pl.multiple_of(start, unit), size)


EVERY = slice(None)


def place_z(blocks, index):
    parts = [
        [
            (
                o,
                (EVERY, slice(o * 128, o * 128 + 128)),
                lambda at: (span((at // 4) * 192, 192, 32), span((at % 4) * 128, 128, 128)),
            )
            for o in range(2)
        ]
    ] * 8
    return place(blocks, index, 0, parts, [(384, 512), (384, 512)])


def around(index):
    return [index, (index + 3) % 4, (index + 1) % 4, (index + 2) % 4]


def place_middle(rows_blocks, columns_blocks, index):
    parts = [[(0, (EVERY, EVERY), lambda at: (span(at * 384, 384, 32), EVERY))]] * 4
    parts += [[(1, (EVERY, EVERY), lambda at: (EVERY, span(at * 512, 512, 128)))]] * 4
    return place([*rows_blocks, *columns_blocks], index, 8, parts, [(1536, 512), (384, 2048)])


def order_tokens(own, other):
    def kernel(own_ref, other_ref, first_ref, second_ref):
        for k, ref in enumerate((own_ref, other_ref)):
            rows = slice(k * 256, k * 256 + 256)
            for zl in range(4):
                for x in range(4):
                    start = (zl * 4 + x) * 256
                    to = zl * 128
                    first_ref[x, rows, to : to + 128] = ref[:, start : start + 128]
                    to += x * 512
                    second_ref[rows, to : to + 128] = ref[:, start + 128 : start + 256]

    vmem = pl.BlockSpec(memory_space=pltpu.VMEM)
    return pl.pallas_call(
        kernel,
        in_specs=[vmem] * 2,
        out_specs=[vmem] * 2,
        out_shape=[jax.ShapeDtypeStruct((4, 512, 512), bf16), jax.ShapeDtypeStruct((512, 2048), bf16)],
        compiler_params=pltpu.CompilerParams(vmem_limit_bytes=VMEM),
    )(own, other)


def swiglu(y, gates, ups, by_step):
    scale = 1.0 / math.sqrt(D)

    def kernel(y_ref, gates_ref, ups_ref, *refs):
        blocks, out_ref = refs[:4], refs[4]

        def write(here):
            for k in range(2):
                cut = slice(k * 384, k * 384 + 384)
                gate = (gates_ref[:, cut] + blocks[(k - here) % 4][...]) * scale
                up = (ups_ref[:, cut] + blocks[(k + 2 - here) % 4][...]) * scale
                out_ref[:, cut] = (jax.nn.silu(gate) * up).astype(bf16)

        for here in range(4):
            pl.when(y_ref[0] == here)(lambda here=here: write(here))

    vmem = pl.BlockSpec(memory_space=pltpu.VMEM)
    return pl.pallas_call(
        kernel,
        in_specs=[pl.BlockSpec(memory_space=pltpu.SMEM)] + [vmem] * 6,
        out_specs=vmem,
        out_shape=jax.ShapeDtypeStruct((512, F), bf16),
        compiler_params=pltpu.CompilerParams(vmem_limit_bytes=VMEM),
    )(y.astype(jnp.int32).reshape(1), gates, ups, *by_step)


def outer_update(delta, master, moment):
    moment_new = outer_momentum * moment + delta
    master_new = master - outer_rate * (delta + outer_momentum * moment_new)
    return master_new, moment_new


def finish(hidden, weights, zh, back, gain_own, gain_other, mixed=None):
    scale = 1.0 / math.sqrt(F)

    def kernel(hidden_ref, weights_ref, back_ref, gain_own_ref, gain_other_ref, *refs):
        out = jnp.dot(hidden_ref[...], weights_ref[...], preferred_element_type=f32) * scale
        out = gain_own_ref[...] * out.astype(bf16).astype(f32)
        out = out + gain_other_ref[...] * back_ref[...].astype(f32)
        refs[-1][...] = out.astype(bf16)

    gain = pl.BlockSpec((256, 1), lambda i: (0, 0))
    more = [] if mixed is None else [mixed]
    return pl.pallas_call(
        kernel,
        grid=(4,),
        in_specs=[
            pl.BlockSpec((256, F), lambda i: (0, 0)),
            pl.BlockSpec((F, 512), lambda i: (zh, i)),
            pl.BlockSpec((256, 512), lambda i: (0, i)),
            gain,
            gain,
        ]
        + [pl.BlockSpec(memory_space=pl.ANY)] * len(more),
        out_specs=pl.BlockSpec((256, 512), lambda i: (0, 2 * i + zh)),
        out_shape=jax.ShapeDtypeStruct((256, 4096), bf16),
        input_output_aliases={5: 0} if more else {},
        compiler_params=pltpu.CompilerParams(vmem_limit_bytes=VMEM),
    )(hidden, weights, back, gain_own, gain_other, *more)


def nt_dot(rows, columns):
    return lax.dot_general(rows, columns, (((1,), (1,)), ((), ())), preferred_element_type=f32)


def body(
    pseudo_in,
    pseudo_out,
    master_in,
    master_out,
    moment_in,
    moment_out,
    tokens,
    route_ids,
    route_weights,
    counts,
):
    core = lax.axis_index("core")
    x = lax.axis_index("x")
    y = lax.axis_index("y")
    zh = lax.axis_index("zh")
    z = zh * 4 + lax.axis_index("zl")
    first_core = core == 0

    own_rows = tokens[0, 0]

    expert_ids = route_ids[0, 0]
    gate_gains = route_weights[0, 0]
    valid_rows = (jnp.arange(256, dtype=jnp.int32) < counts[0, 0]).astype(f32)
    gain_own = valid_rows * jnp.sum(gate_gains * (expert_ids == core).astype(f32), axis=1)
    gain_other = valid_rows * jnp.sum(gate_gains * (expert_ids != core).astype(f32), axis=1)

    def rows_of(a_in, a_out):
        return jnp.concatenate([a_in.transpose(0, 2, 1), a_out], axis=1)

    states = jnp.stack([rows_of(master_in, master_out), rows_of(moment_in, moment_out)], axis=1)

    grads_in = pseudo_in[0].astype(bf16).transpose(0, 2, 1).reshape(2, 8, 192, 256)
    grads_out = (
        pseudo_out[0].astype(bf16).reshape(2, 48, 8, 2, 256).transpose(0, 2, 3, 1, 4).reshape(2, 8, 96, 256)
    )
    grads = jnp.concatenate([grads_in, grads_out], axis=2)
    got = core_swap(pick(grads, 1 - core))
    total = (pick(grads, core).astype(f32) + got.astype(f32)).reshape(4, 2, 288, 256)
    low = total.astype(bf16)
    index = jnp.stack(
        [(z + k) % 8 for k in (0, 7, 6, 5, 1, 2, 3, 4)] + around(y) + around(x)
    ).astype(jnp.int32)
    *sends, kept, token_rows, states, index = together(
        *[pick(low, (y + k) % 4) for k in (1, 3, 2)], pick(total, y), own_rows, states, index
    )
    *got, other_rows, state_got, index, gain_own, gain_other = together(
        *[moved(s, "y", k) for s, k in zip(sends, (1, 3, 2))],
        core_swap(token_rows),
        core_swap(pick(states, 1 - core)),
        index,
        gain_own[:, None],
        gain_other[:, None],
    )
    for g in got:
        kept = kept + g.astype(f32)
    state_own = pick(states, core)
    send, kept, state_own, state_got = together(
        pick(kept, 1 - zh).astype(bf16), pick(kept, zh), state_own, state_got
    )
    state = jnp.where(
        first_core, jnp.stack([state_own, state_got], 1), jnp.stack([state_got, state_own], 1)
    )
    got, state = together(moved(send, "z", 4), state)
    delta = (kept + got.astype(f32)) / REPLICAS
    new_master_a, new_moment_a = outer_update(
        delta[:192].reshape(2, 96, 256), state[0, :, :96], state[1, :, :96]
    )
    new_master_b, new_moment_b = outer_update(
        delta[192:].reshape(2, 48, 256), state[0, :, 96:], state[1, :, 96:]
    )

    w_in = new_master_a.astype(bf16).reshape(192, 256)
    w_out = new_master_b.astype(bf16).reshape(96, 256)
    w_in, w_out, token_rows, other_rows = together(w_in, w_out, token_rows, other_rows)
    rows = order_tokens(token_rows, other_rows)
    b_1, f_1, f_4, *rest = together(
        moved(w_in, "z", 1),
        moved(w_in, "z", -1),
        moved(w_in, "z", 4),
        *[moved(w_out, "y", k) for k in (1, -1, 2)],
        *rows,
    )
    o, rows = rest[:3], rest[3:]
    parts = [
        [
            (0, (slice(c * 48, c * 48 + 48), EVERY), lambda at, c=c: (EVERY, span(at * 512 + c * 256, 256, 128)))
            for c in range(2)
        ]
    ] * 4
    p2 = place([w_out, *o], index, 8, parts, [(48, 2048)])[0]
    b_1, f_1, f_4, p2 = together(b_1, f_1, f_4, p2)
    b_2, f_3, f_2, b_3, *o = together(
        moved(b_1, "z", 1),
        moved(f_4, "z", 1),
        moved(f_1, "z", -1),
        moved(f_4, "z", -1),
        *[moved(p2, "x", k) for k in (1, -1, 2)],
    )
    parts = [[(0, (EVERY, EVERY), lambda at: (span(at * 48, 48, 16), EVERY))]] * 4
    p2 = place([p2, *o], index, 12, parts, [(192, 2048)])[0]
    p0, p1 = place_z([w_in, b_1, b_2, b_3, f_1, f_2, f_3, f_4], index)
    p0, p1, p2 = together(p0, p1, p2)
    weights_out = lax.all_gather(p2, ("zh", "zl"), tiled=True)

    updated = jnp.stack(
        [
            jnp.concatenate([new_master_a, new_master_b], axis=1),
            jnp.concatenate([new_moment_a, new_moment_b], axis=1),
        ],
        axis=1,
    )
    *o, updated = together(
        *[moved(p0, "y", k) for k in (1, -1, 2)], *[moved(p1, "x", k) for k in (1, -1, 2)], updated
    )
    p0, p1 = place_middle([p0, *o[:3]], [p1, *o[3:]], index)
    p0, p1, updated = together(p0, p1, updated)
    rows_0, rows_1 = rows

    def x_dot(step, block):
        return nt_dot(pick(rows_0, (x + step) % 4), block)

    mine = pick(updated, core)
    x_l, x_r, y_l, y_r, mine, got, total, here = together(
        moved(p0, "x", 1),
        moved(p0, "x", -1),
        moved(p1, "y", 1),
        moved(p1, "y", -1),
        mine,
        core_swap(pick(updated, 1 - core)),
        x_dot(0, p0),
        nt_dot(rows_1, p1),
    )
    final = jnp.where(first_core, jnp.stack([mine, got], 1), jnp.stack([got, mine], 1))
    new_in, new_out = final[:, :, :96].transpose(0, 1, 3, 2), final[:, :, 96:]
    (total,) = together(total + x_dot(3, x_l))
    total = total + x_dot(1, x_r)
    x_o, x_o2, y_o, y_o2, total, before, after, new_in, new_out, weights_out = together(
        moved(x_l[:768], "x", 1),
        moved(x_r[768:], "x", -1),
        moved(y_l[:192], "y", 1),
        moved(y_r[192:], "y", -1),
        total,
        nt_dot(rows_1, y_l),
        nt_dot(rows_1, y_r),
        new_in,
        new_out,
        weights_out,
    )
    halves = [total[:, :F] + x_dot(2, x_o), total[:, F:] + x_dot(2, x_o2)]
    across = jnp.concatenate([nt_dot(rows_1, y_o), nt_dot(rows_1, y_o2)], axis=1)
    hidden = swiglu(y, *halves, [here, after, across, before])

    scale_out = 1.0 / math.sqrt(F)
    back = []
    for k in range(2):
        out = jnp.dot(hidden[256:], weights_out[k * F : k * F + F], preferred_element_type=f32)
        back.append(core_swap((out * scale_out).astype(bf16)))
    mixed = finish(hidden, weights_out, 0, back[0], gain_own, gain_other)
    mixed = finish(hidden, weights_out, 1, back[1], gain_own, gain_other, mixed)

    return new_in[0], new_out[0], new_in[1], new_out[1], mixed[None, None]


def solution(mesh):
    fine = Mesh(mesh.devices.reshape(SIZES), AXES)
    replica, shard = ("y", "zh", "core"), ("zl", "x")
    state = P(None, shard, replica)
    in_specs = (
        P(replica, None, shard, None),
        P(replica, None, shard, None),
        state,
        state,
        state,
        state,
        P(replica, shard, None, None),
        P(replica, shard, None, None),
        P(replica, shard, None, None),
        P(replica, shard),
    )
    out_specs = (state, state, state, state, P(replica, shard, None, None))
    return jax.shard_map(body, mesh=fine, in_specs=in_specs, out_specs=out_specs, check_vma=False)
```

```python
import itertools
import math

import jax
import jax.numpy as jnp
from jax import lax
from jax.experimental import pallas as pl
from jax.experimental.pallas import tpu as pltpu
from jax.sharding import Mesh
from jax.sharding import PartitionSpec as P

D = 4096
F = 768
REPLICAS = 16

outer_rate = 0.7
outer_momentum = 0.9

AXES = ("y", "zh", "core", "zl", "x")
SIZES = (4, 2, 2, 4, 4)
PLACES = list(itertools.product(*(range(n) for n in SIZES)))
NUMBER = {place: i for i, place in enumerate(PLACES)}
LENGTH = {"x": 4, "y": 4, "z": 8}
VMEM = 12 * 2**20
bf16 = jnp.bfloat16
f32 = jnp.float32


def moved(block, axis, step):
    route = []
    for y, zh, core, zl, x in PLACES:
        z = zh * 4 + zl
        if axis == "x":
            x2, y2, z2 = (x + step) % 4, y, z
        elif axis == "y":
            x2, y2, z2 = x, (y + step) % 4, z
        else:
            x2, y2, z2 = x, y, (z + step) % 8
        route.append((NUMBER[(y, zh, core, zl, x)], NUMBER[(y2, z2 // 4, core, z2 % 4, x2)]))
    return lax.ppermute(block, AXES, route)


def core_swap(block):
    return lax.ppermute(block, "core", [(0, 1), (1, 0)])


def pick(array, index):
    return lax.dynamic_index_in_dim(array, index, 0, keepdims=False)


def together(*arrays):
    return lax.optimization_barrier(tuple(arrays))


def place(blocks, index, positions, parts, out_shapes):
    count = len(blocks)

    def kernel(index_ref, *refs):
        ins, outs = refs[:count], refs[count:]
        for j in range(count):
            at = index_ref[positions[j]]
            for o, source, target in parts[j]:
                outs[o][target(at)] = ins[j][source]

    vmem = pl.BlockSpec(memory_space=pltpu.VMEM)
    return pl.pallas_call(
        kernel,
        in_specs=[pl.BlockSpec(memory_space=pltpu.SMEM)] + [vmem] * count,
        out_specs=[vmem] * len(out_shapes),
        out_shape=[jax.ShapeDtypeStruct(s, bf16) for s in out_shapes],
        compiler_params=pltpu.CompilerParams(vmem_limit_bytes=VMEM),
    )(index, *blocks)


def span(start, size, unit):
    return pl.ds(pl.multiple_of(start, unit), size)


EVERY = slice(None)


def place_first(z_blocks, x_blocks, index):
    parts = [
        [
            (
                o,
                (EVERY, slice(o * 128, o * 128 + 128)),
                lambda at: (span((at // 4) * 192, 192, 32), span((at % 4) * 128, 128, 128)),
            )
            for o in range(2)
        ]
    ] * 8
    parts += [[(2, (EVERY, EVERY), lambda at: (span(at * 48, 48, 16), EVERY))]] * 4
    positions = [*range(8), *range(12, 16)]
    return place(
        [*z_blocks, *x_blocks], index, positions, parts, [(384, 512), (384, 512), (192, 2048)]
    )


def around(index):
    return [index, (index + 3) % 4, (index + 1) % 4, (index + 2) % 4]


def place_middle(rows_blocks, columns_blocks, index):
    parts = [[(0, (EVERY, EVERY), lambda at: (span(at * 384, 384, 32), EVERY))]] * 4
    parts += [[(1, (EVERY, EVERY), lambda at: (EVERY, span(at * 512, 512, 128)))]] * 4
    return place(
        [*rows_blocks, *columns_blocks], index, range(8, 16), parts, [(1536, 512), (384, 2048)]
    )


def order_tokens(own, other, index):
    def kernel(index_ref, own_ref, other_ref, *outs):
        for k, ref in enumerate((own_ref, other_ref)):
            rows = slice(k * 256, k * 256 + 256)
            for zl in range(4):
                for j in range(4):
                    start = (zl * 4 + index_ref[12 + j]) * 256
                    outs[j][rows, zl * 128 : zl * 128 + 128] = ref[:, span(start, 128, 128)]
                    start = (zl * 4 + j) * 256 + 128
                    to = (j * 4 + zl) * 128
                    outs[4][rows, to : to + 128] = ref[:, start : start + 128]

    vmem = pl.BlockSpec(memory_space=pltpu.VMEM)
    return pl.pallas_call(
        kernel,
        in_specs=[pl.BlockSpec(memory_space=pltpu.SMEM)] + [vmem] * 2,
        out_specs=[vmem] * 5,
        out_shape=[jax.ShapeDtypeStruct(s, bf16) for s in [(512, 512)] * 4 + [(512, 2048)]],
        compiler_params=pltpu.CompilerParams(vmem_limit_bytes=VMEM),
    )(index, own, other)


def swiglu(y, gates, ups, by_step):
    scale = 1.0 / math.sqrt(D)

    def kernel(y_ref, gates_ref, ups_ref, *refs):
        blocks, out_ref = refs[:4], refs[4]

        def write(here):
            for k in range(2):
                cut = slice(k * 384, k * 384 + 384)
                gate = (gates_ref[:, cut] + blocks[(k - here) % 4][...]) * scale
                up = (ups_ref[:, cut] + blocks[(k + 2 - here) % 4][...]) * scale
                out_ref[:, cut] = (jax.nn.silu(gate) * up).astype(bf16)

        for here in range(4):
            pl.when(y_ref[0] == here)(lambda here=here: write(here))

    vmem = pl.BlockSpec(memory_space=pltpu.VMEM)
    return pl.pallas_call(
        kernel,
        in_specs=[pl.BlockSpec(memory_space=pltpu.SMEM)] + [vmem] * 6,
        out_specs=vmem,
        out_shape=jax.ShapeDtypeStruct((512, F), bf16),
        compiler_params=pltpu.CompilerParams(vmem_limit_bytes=VMEM),
    )(y.astype(jnp.int32).reshape(1), gates, ups, *by_step)


def outer_update(delta, master, moment):
    moment_new = outer_momentum * moment + delta
    master_new = master - outer_rate * (delta + outer_momentum * moment_new)
    return master_new, moment_new


def finish(hidden, weights, zh, back, gain_own, gain_other, mixed=None):
    scale = 1.0 / math.sqrt(F)

    def kernel(hidden_ref, weights_ref, back_ref, gain_own_ref, gain_other_ref, *refs):
        out = jnp.dot(hidden_ref[...], weights_ref[...], preferred_element_type=f32) * scale
        out = gain_own_ref[...] * out.astype(bf16).astype(f32)
        out = out + gain_other_ref[...] * back_ref[...].astype(f32)
        refs[-1][...] = out.astype(bf16)

    gain = pl.BlockSpec((256, 1), lambda i: (0, 0))
    more = [] if mixed is None else [mixed]
    return pl.pallas_call(
        kernel,
        grid=(4,),
        in_specs=[
            pl.BlockSpec((256, F), lambda i: (0, 0)),
            pl.BlockSpec((F, 512), lambda i: (zh, i)),
            pl.BlockSpec((256, 512), lambda i: (0, i)),
            gain,
            gain,
        ]
        + [pl.BlockSpec(memory_space=pl.ANY)] * len(more),
        out_specs=pl.BlockSpec((256, 512), lambda i: (0, 2 * i + zh)),
        out_shape=jax.ShapeDtypeStruct((256, 4096), bf16),
        input_output_aliases={5: 0} if more else {},
        compiler_params=pltpu.CompilerParams(vmem_limit_bytes=VMEM),
    )(hidden, weights, back, gain_own, gain_other, *more)


def nt_dot(rows, columns):
    return lax.dot_general(rows, columns, (((1,), (1,)), ((), ())), preferred_element_type=f32)


def body(
    pseudo_in,
    pseudo_out,
    master_in,
    master_out,
    moment_in,
    moment_out,
    tokens,
    route_ids,
    route_weights,
    counts,
):
    core = lax.axis_index("core")
    x = lax.axis_index("x")
    y = lax.axis_index("y")
    zh = lax.axis_index("zh")
    z = zh * 4 + lax.axis_index("zl")
    first_core = core == 0

    own_rows = tokens[0, 0]

    expert_ids = route_ids[0, 0]
    gate_gains = route_weights[0, 0]
    valid_rows = (jnp.arange(256, dtype=jnp.int32) < counts[0, 0]).astype(f32)
    gain_own = valid_rows * jnp.sum(gate_gains * (expert_ids == core).astype(f32), axis=1)
    gain_other = valid_rows * jnp.sum(gate_gains * (expert_ids != core).astype(f32), axis=1)

    def rows_of(a_in, a_out):
        return jnp.concatenate([a_in.transpose(0, 2, 1), a_out], axis=1)

    states = jnp.stack([rows_of(master_in, master_out), rows_of(moment_in, moment_out)], axis=1)

    def columns_first(a_in, a_out):
        a_in = a_in.T.reshape(8, 192, 256)
        return a_in, a_out.reshape(48, 8, 2, 256).transpose(1, 2, 0, 3).reshape(8, 96, 256)

    others = [pick(p[0], 1 - core).astype(bf16) for p in (pseudo_in, pseudo_out)]
    got = core_swap(jnp.concatenate(columns_first(*others), axis=1))
    own_in, own_out = columns_first(pick(pseudo_in[0], core), pick(pseudo_out[0], core))
    total = jnp.concatenate([own_in, own_out], axis=1) + got.astype(f32)
    total = total.reshape(4, 2, 288, 256)
    low = total.astype(bf16)
    index = jnp.stack(
        [(z + k) % 8 for k in (0, 7, 6, 5, 1, 2, 3, 4)] + around(y) + around(x)
    ).astype(jnp.int32)
    *sends, kept, token_rows, states, index = together(
        *[pick(low, (y + k) % 4) for k in (1, 3, 2)], pick(total, y), own_rows, states, index
    )
    *got, other_rows, state_got, index, gain_own, gain_other = together(
        *[moved(s, "y", k) for s, k in zip(sends, (1, 3, 2))],
        core_swap(token_rows),
        core_swap(pick(states, 1 - core)),
        index,
        gain_own[:, None],
        gain_other[:, None],
    )
    for g in got:
        kept = kept + g.astype(f32)
    state_own = pick(states, core)
    send, kept, state_own, state_got = together(
        pick(kept, 1 - zh).astype(bf16), pick(kept, zh), state_own, state_got
    )
    state = jnp.where(
        first_core, jnp.stack([state_own, state_got], 1), jnp.stack([state_got, state_own], 1)
    )
    got, state = together(moved(send, "z", 4), state)
    delta = (kept + got.astype(f32)) / REPLICAS
    new_master_a, new_moment_a = outer_update(
        delta[:192].reshape(2, 96, 256), state[0, :, :96], state[1, :, :96]
    )
    new_master_b, new_moment_b = outer_update(
        delta[192:].reshape(2, 48, 256), state[0, :, 96:], state[1, :, 96:]
    )

    w_in = new_master_a.astype(bf16).reshape(192, 256)
    w_out = new_master_b.astype(bf16).reshape(96, 256)
    w_in, w_out, token_rows, other_rows = together(w_in, w_out, token_rows, other_rows)
    rows = order_tokens(token_rows, other_rows, index)
    b_1, f_1, f_4, *rest = together(
        moved(w_in, "z", 1),
        moved(w_in, "z", -1),
        moved(w_in, "z", 4),
        *[moved(w_out, "y", k) for k in (1, -1, 2)],
        *rows,
    )
    o, rows = rest[:3], rest[3:]
    parts = [
        [
            (0, (slice(c * 48, c * 48 + 48), EVERY), lambda at, c=c: (EVERY, span(at * 512 + c * 256, 256, 128)))
            for c in range(2)
        ]
    ] * 4
    p2 = place([w_out, *o], index, range(8, 12), parts, [(48, 2048)])[0]
    b_1, f_1, f_4, p2 = together(b_1, f_1, f_4, p2)
    b_2, f_3, f_2, b_3, *o = together(
        moved(b_1, "z", 1),
        moved(f_4, "z", 1),
        moved(f_1, "z", -1),
        moved(f_4, "z", -1),
        *[moved(p2, "x", k) for k in (1, -1, 2)],
    )
    p0, p1, p2 = place_first([w_in, b_1, b_2, b_3, f_1, f_2, f_3, f_4], [p2, *o], index)
    p0, p1, p2 = together(p0, p1, p2)
    weights_out = lax.all_gather(p2, ("zh", "zl"), tiled=True)

    o = together(*[moved(p0, "y", k) for k in (1, -1, 2)], *[moved(p1, "x", k) for k in (1, -1, 2)])
    p0, p1 = place_middle([p0, *o[:3]], [p1, *o[3:]], index)
    p0, p1, new_master_a, new_moment_a, new_master_b, new_moment_b = together(
        p0, p1, new_master_a, new_moment_a, new_master_b, new_moment_b
    )
    rows_here, rows_before, rows_after, rows_across, rows_1 = rows

    updated = jnp.stack(
        [
            jnp.concatenate([new_master_a, new_master_b], axis=1),
            jnp.concatenate([new_moment_a, new_moment_b], axis=1),
        ],
        axis=1,
    )
    mine = pick(updated, core)
    x_l, x_r, y_l, y_r, mine, got, total, here = together(
        moved(p0, "x", 1),
        moved(p0, "x", -1),
        moved(p1, "y", 1),
        moved(p1, "y", -1),
        mine,
        core_swap(pick(updated, 1 - core)),
        nt_dot(rows_here, p0),
        nt_dot(rows_1, p1),
    )
    final = jnp.where(first_core, jnp.stack([mine, got], 1), jnp.stack([got, mine], 1))
    new_in, new_out = final[:, :, :96].transpose(0, 1, 3, 2), final[:, :, 96:]
    (total,) = together(total + nt_dot(rows_before, x_l))
    total = total + nt_dot(rows_after, x_r)
    x_o, x_o2, y_o, y_o2, total, before, after, new_in, new_out, weights_out = together(
        moved(x_l[:768], "x", 1),
        moved(x_r[768:], "x", -1),
        moved(y_l[:192], "y", 1),
        moved(y_r[192:], "y", -1),
        total,
        nt_dot(rows_1, y_l),
        nt_dot(rows_1, y_r),
        new_in,
        new_out,
        weights_out,
    )
    halves = [total[:, :F] + nt_dot(rows_across, x_o), total[:, F:] + nt_dot(rows_across, x_o2)]
    across = jnp.concatenate([nt_dot(rows_1, y_o), nt_dot(rows_1, y_o2)], axis=1)
    hidden = swiglu(y, *halves, [here, after, across, before])

    scale_out = 1.0 / math.sqrt(F)
    back = []
    for k in range(2):
        out = jnp.dot(hidden[256:], weights_out[k * F : k * F + F], preferred_element_type=f32)
        back.append(core_swap((out * scale_out).astype(bf16)))
    mixed = finish(hidden, weights_out, 0, back[0], gain_own, gain_other)
    mixed = finish(hidden, weights_out, 1, back[1], gain_own, gain_other, mixed)

    return new_in[0], new_out[0], new_in[1], new_out[1], mixed[None, None]


def solution(mesh):
    fine = Mesh(mesh.devices.reshape(SIZES), AXES)
    replica, shard = ("y", "zh", "core"), ("zl", "x")
    state = P(None, shard, replica)
    in_specs = (
        P(replica, None, shard, None),
        P(replica, None, shard, None),
        state,
        state,
        state,
        state,
        P(replica, shard, None, None),
        P(replica, shard, None, None),
        P(replica, shard, None, None),
        P(replica, shard),
    )
    out_specs = (state, state, state, state, P(replica, shard, None, None))
    return jax.shard_map(body, mesh=fine, in_specs=in_specs, out_specs=out_specs, check_vma=False)
```

```python
import itertools
import math

import jax
import jax.numpy as jnp
from jax import lax
from jax.experimental import pallas as pl
from jax.experimental.pallas import tpu as pltpu
from jax.sharding import Mesh
from jax.sharding import PartitionSpec as P

D = 4096
F = 768
REPLICAS = 16

outer_rate = 0.7
outer_momentum = 0.9

AXES = ("y", "zh", "core", "zl", "x")
SIZES = (4, 2, 2, 4, 4)
PLACES = list(itertools.product(*(range(n) for n in SIZES)))
NUMBER = {place: i for i, place in enumerate(PLACES)}
LENGTH = {"x": 4, "y": 4, "z": 8}
VMEM = 12 * 2**20
bf16 = jnp.bfloat16
f32 = jnp.float32


def moved(block, axis, step):
    route = []
    for y, zh, core, zl, x in PLACES:
        z = zh * 4 + zl
        if axis == "x":
            x2, y2, z2 = (x + step) % 4, y, z
        elif axis == "y":
            x2, y2, z2 = x, (y + step) % 4, z
        else:
            x2, y2, z2 = x, y, (z + step) % 8
        route.append((NUMBER[(y, zh, core, zl, x)], NUMBER[(y2, z2 // 4, core, z2 % 4, x2)]))
    return lax.ppermute(block, AXES, route)


def core_swap(block):
    return lax.ppermute(block, "core", [(0, 1), (1, 0)])


def pick(array, index):
    return lax.dynamic_index_in_dim(array, index, 0, keepdims=False)


def together(*arrays):
    return lax.optimization_barrier(tuple(arrays))


def place(blocks, index, positions, parts, out_shapes):
    count = len(blocks)

    def kernel(index_ref, *refs):
        ins, outs = refs[:count], refs[count:]
        for j in range(count):
            at = index_ref[positions[j]]
            for o, source, target in parts[j]:
                outs[o][target(at)] = ins[j][source]

    vmem = pl.BlockSpec(memory_space=pltpu.VMEM)
    return pl.pallas_call(
        kernel,
        in_specs=[pl.BlockSpec(memory_space=pltpu.SMEM)] + [vmem] * count,
        out_specs=[vmem] * len(out_shapes),
        out_shape=[jax.ShapeDtypeStruct(s, bf16) for s in out_shapes],
        compiler_params=pltpu.CompilerParams(vmem_limit_bytes=VMEM),
    )(index, *blocks)


def span(start, size, unit):
    return pl.ds(pl.multiple_of(start, unit), size)


EVERY = slice(None)


def place_first(z_blocks, x_blocks, index):
    parts = [
        [
            (
                o,
                (EVERY, slice(o * 128, o * 128 + 128)),
                lambda at: (span((at // 4) * 192, 192, 32), span((at % 4) * 128, 128, 128)),
            )
            for o in range(2)
        ]
    ] * 8
    parts += [[(2, (EVERY, EVERY), lambda at: (span(at * 48, 48, 16), EVERY))]] * 4
    positions = [*range(8), *range(12, 16)]
    return place(
        [*z_blocks, *x_blocks], index, positions, parts, [(384, 512), (384, 512), (192, 2048)]
    )


def around(index):
    return [index, (index + 3) % 4, (index + 1) % 4, (index + 2) % 4]


def place_middle(rows_blocks, columns_blocks, index):
    parts = [[(0, (EVERY, EVERY), lambda at: (span(at * 384, 384, 32), EVERY))]] * 4
    parts += [[(1, (EVERY, EVERY), lambda at: (EVERY, span(at * 512, 512, 128)))]] * 4
    return place(
        [*rows_blocks, *columns_blocks], index, range(8, 16), parts, [(1536, 512), (384, 2048)]
    )


def order_tokens(own, other, index):
    def kernel(index_ref, own_ref, other_ref, *outs):
        for k, ref in enumerate((own_ref, other_ref)):
            rows = slice(k * 256, k * 256 + 256)
            for zl in range(4):
                for j in range(4):
                    start = (zl * 4 + index_ref[12 + j]) * 256
                    outs[j][rows, zl * 128 : zl * 128 + 128] = ref[:, span(start, 128, 128)]
                    start = (zl * 4 + j) * 256 + 128
                    to = (j * 4 + zl) * 128
                    outs[4][rows, to : to + 128] = ref[:, start : start + 128]

    vmem = pl.BlockSpec(memory_space=pltpu.VMEM)
    return pl.pallas_call(
        kernel,
        in_specs=[pl.BlockSpec(memory_space=pltpu.SMEM)] + [vmem] * 2,
        out_specs=[vmem] * 5,
        out_shape=[jax.ShapeDtypeStruct(s, bf16) for s in [(512, 512)] * 4 + [(512, 2048)]],
        compiler_params=pltpu.CompilerParams(vmem_limit_bytes=VMEM),
    )(index, own, other)


def swiglu(y, gates, ups, by_step):
    scale = 1.0 / math.sqrt(D)

    def kernel(y_ref, gates_ref, ups_ref, *refs):
        blocks, out_ref = refs[:4], refs[4]

        def write(here):
            for k in range(2):
                cut = slice(k * 384, k * 384 + 384)
                gate = (gates_ref[:, cut] + blocks[(k - here) % 4][...]) * scale
                up = (ups_ref[:, cut] + blocks[(k + 2 - here) % 4][...]) * scale
                out_ref[:, cut] = (jax.nn.silu(gate) * up).astype(bf16)

        for here in range(4):
            pl.when(y_ref[0] == here)(lambda here=here: write(here))

    vmem = pl.BlockSpec(memory_space=pltpu.VMEM)
    return pl.pallas_call(
        kernel,
        in_specs=[pl.BlockSpec(memory_space=pltpu.SMEM)] + [vmem] * 6,
        out_specs=vmem,
        out_shape=jax.ShapeDtypeStruct((512, F), bf16),
        compiler_params=pltpu.CompilerParams(vmem_limit_bytes=VMEM),
    )(y.astype(jnp.int32).reshape(1), gates, ups, *by_step)


def outer_update(delta, master, moment):
    moment_new = outer_momentum * moment + delta
    master_new = master - outer_rate * (delta + outer_momentum * moment_new)
    return master_new, moment_new


def finish(hidden, weights, zh, back, gain_own, gain_other, mixed=None):
    scale = 1.0 / math.sqrt(F)

    def kernel(hidden_ref, weights_ref, back_ref, gain_own_ref, gain_other_ref, *refs):
        out = jnp.dot(hidden_ref[...], weights_ref[...], preferred_element_type=f32) * scale
        out = gain_own_ref[...] * out.astype(bf16).astype(f32)
        out = out + gain_other_ref[...] * back_ref[...].astype(f32)
        refs[-1][...] = out.astype(bf16)

    gain = pl.BlockSpec((256, 1), lambda i: (0, 0))
    more = [] if mixed is None else [mixed]
    return pl.pallas_call(
        kernel,
        grid=(4,),
        in_specs=[
            pl.BlockSpec((256, F), lambda i: (0, 0)),
            pl.BlockSpec((F, 512), lambda i: (zh, i)),
            pl.BlockSpec((256, 512), lambda i: (0, i)),
            gain,
            gain,
        ]
        + [pl.BlockSpec(memory_space=pl.ANY)] * len(more),
        out_specs=pl.BlockSpec((256, 512), lambda i: (0, 2 * i + zh)),
        out_shape=jax.ShapeDtypeStruct((256, 4096), bf16),
        input_output_aliases={5: 0} if more else {},
        compiler_params=pltpu.CompilerParams(vmem_limit_bytes=VMEM),
    )(hidden, weights, back, gain_own, gain_other, *more)


def nt_dot(rows, columns):
    return lax.dot_general(rows, columns, (((1,), (1,)), ((), ())), preferred_element_type=f32)


def body(
    pseudo_in,
    pseudo_out,
    master_in,
    master_out,
    moment_in,
    moment_out,
    tokens,
    route_ids,
    route_weights,
    counts,
):
    core = lax.axis_index("core")
    x = lax.axis_index("x")
    y = lax.axis_index("y")
    zh = lax.axis_index("zh")
    z = zh * 4 + lax.axis_index("zl")
    first_core = core == 0

    own_rows = tokens[0, 0]

    expert_ids = route_ids[0, 0]
    gate_gains = route_weights[0, 0]
    valid_rows = (jnp.arange(256, dtype=jnp.int32) < counts[0, 0]).astype(f32)
    gain_own = valid_rows * jnp.sum(gate_gains * (expert_ids == core).astype(f32), axis=1)
    gain_other = valid_rows * jnp.sum(gate_gains * (expert_ids != core).astype(f32), axis=1)

    def rows_of(a_in, a_out):
        return jnp.concatenate([a_in.transpose(0, 2, 1), a_out], axis=1)

    states = jnp.stack([rows_of(master_in, master_out), rows_of(moment_in, moment_out)], axis=1)

    grads_in = pseudo_in[0].astype(bf16).transpose(0, 2, 1).reshape(2, 8, 192, 256)
    grads_out = (
        pseudo_out[0].astype(bf16).reshape(2, 48, 8, 2, 256).transpose(0, 2, 3, 1, 4).reshape(2, 8, 96, 256)
    )
    grads = jnp.concatenate([grads_in, grads_out], axis=2)
    got = core_swap(pick(grads, 1 - core))
    total = (pick(grads, core).astype(f32) + got.astype(f32)).reshape(4, 2, 288, 256)
    low = total.astype(bf16)
    index = jnp.stack(
        [(z + k) % 8 for k in (0, 7, 6, 5, 1, 2, 3, 4)] + around(y) + around(x)
    ).astype(jnp.int32)
    *sends, kept, token_rows, states, index = together(
        *[pick(low, (y + k) % 4) for k in (1, 3, 2)], pick(total, y), own_rows, states, index
    )
    *got, other_rows, state_got, index, gain_own, gain_other = together(
        *[moved(s, "y", k) for s, k in zip(sends, (1, 3, 2))],
        core_swap(token_rows),
        core_swap(pick(states, 1 - core)),
        index,
        gain_own[:, None],
        gain_other[:, None],
    )
    for g in got:
        kept = kept + g.astype(f32)
    state_own = pick(states, core)
    send, kept, state_own, state_got = together(
        pick(kept, 1 - zh).astype(bf16), pick(kept, zh), state_own, state_got
    )
    state = jnp.where(
        first_core, jnp.stack([state_own, state_got], 1), jnp.stack([state_got, state_own], 1)
    )
    got, state = together(moved(send, "z", 4), state)
    delta = (kept + got.astype(f32)) / REPLICAS
    new_master_a, new_moment_a = outer_update(
        delta[:192].reshape(2, 96, 256), state[0, :, :96], state[1, :, :96]
    )
    new_master_b, new_moment_b = outer_update(
        delta[192:].reshape(2, 48, 256), state[0, :, 96:], state[1, :, 96:]
    )

    w_in = new_master_a.astype(bf16).reshape(192, 256)
    w_out = new_master_b.astype(bf16).reshape(96, 256)
    w_in, w_out = together(w_in, w_out)
    b_1, f_1, f_4, *o = together(
        moved(w_in, "z", 1),
        moved(w_in, "z", -1),
        moved(w_in, "z", 4),
        *[moved(w_out, "y", k) for k in (1, -1, 2)],
    )
    parts = [
        [
            (0, (slice(c * 48, c * 48 + 48), EVERY), lambda at, c=c: (EVERY, span(at * 512 + c * 256, 256, 128)))
            for c in range(2)
        ]
    ] * 4
    p2 = place([w_out, *o], index, range(8, 12), parts, [(48, 2048)])[0]
    b_1, f_1, f_4, p2 = together(b_1, f_1, f_4, p2)
    b_2, f_3, f_2, b_3, *o = together(
        moved(b_1, "z", 1),
        moved(f_4, "z", 1),
        moved(f_1, "z", -1),
        moved(f_4, "z", -1),
        *[moved(p2, "x", k) for k in (1, -1, 2)],
    )
    p0, p1, p2 = place_first([w_in, b_1, b_2, b_3, f_1, f_2, f_3, f_4], [p2, *o], index)
    p0, p1, p2 = together(p0, p1, p2)
    weights_out = lax.all_gather(p2, ("zh", "zl"), tiled=True)

    o = together(*[moved(p0, "y", k) for k in (1, -1, 2)], *[moved(p1, "x", k) for k in (1, -1, 2)])
    p0, p1 = place_middle([p0, *o[:3]], [p1, *o[3:]], index)
    p0, p1, new_master_a, new_moment_a, new_master_b, new_moment_b, token_rows, other_rows = together(
        p0, p1, new_master_a, new_moment_a, new_master_b, new_moment_b, token_rows, other_rows
    )
    rows_here, rows_before, rows_after, rows_across, rows_1 = order_tokens(token_rows, other_rows, index)

    updated = jnp.stack(
        [
            jnp.concatenate([new_master_a, new_master_b], axis=1),
            jnp.concatenate([new_moment_a, new_moment_b], axis=1),
        ],
        axis=1,
    )
    mine = pick(updated, core)
    x_l, x_r, y_l, y_r, mine, got, total, here = together(
        moved(p0, "x", 1),
        moved(p0, "x", -1),
        moved(p1, "y", 1),
        moved(p1, "y", -1),
        mine,
        core_swap(pick(updated, 1 - core)),
        nt_dot(rows_here, p0),
        nt_dot(rows_1, p1),
    )
    final = jnp.where(first_core, jnp.stack([mine, got], 1), jnp.stack([got, mine], 1))
    new_in, new_out = final[:, :, :96].transpose(0, 1, 3, 2), final[:, :, 96:]
    (total,) = together(total + nt_dot(rows_before, x_l))
    total = total + nt_dot(rows_after, x_r)
    x_o, x_o2, y_o, y_o2, total, before, after, new_in, new_out = together(
        moved(x_l[:768], "x", 1),
        moved(x_r[768:], "x", -1),
        moved(y_l[:192], "y", 1),
        moved(y_r[192:], "y", -1),
        total,
        nt_dot(rows_1, y_l),
        nt_dot(rows_1, y_r),
        new_in,
        new_out,
    )
    halves = [total[:, :F] + nt_dot(rows_across, x_o), total[:, F:] + nt_dot(rows_across, x_o2)]
    across = jnp.concatenate([nt_dot(rows_1, y_o), nt_dot(rows_1, y_o2)], axis=1)
    hidden = swiglu(y, *halves, [here, after, across, before])

    scale_out = 1.0 / math.sqrt(F)
    back = []
    for k in range(2):
        out = jnp.dot(hidden[256:], weights_out[k * F : k * F + F], preferred_element_type=f32)
        back.append(core_swap((out * scale_out).astype(bf16)))
    mixed = finish(hidden, weights_out, 0, back[0], gain_own, gain_other)
    mixed = finish(hidden, weights_out, 1, back[1], gain_own, gain_other, mixed)

    return new_in[0], new_out[0], new_in[1], new_out[1], mixed[None, None]


def solution(mesh):
    fine = Mesh(mesh.devices.reshape(SIZES), AXES)
    replica, shard = ("y", "zh", "core"), ("zl", "x")
    state = P(None, shard, replica)
    in_specs = (
        P(replica, None, shard, None),
        P(replica, None, shard, None),
        state,
        state,
        state,
        state,
        P(replica, shard, None, None),
        P(replica, shard, None, None),
        P(replica, shard, None, None),
        P(replica, shard),
    )
    out_specs = (state, state, state, state, P(replica, shard, None, None))
    return jax.shard_map(body, mesh=fine, in_specs=in_specs, out_specs=out_specs, check_vma=False)
```

```python
import itertools
import math

import jax
import jax.numpy as jnp
from jax import lax
from jax.experimental import pallas as pl
from jax.experimental.pallas import tpu as pltpu
from jax.sharding import Mesh
from jax.sharding import PartitionSpec as P

D = 4096
F = 768
REPLICAS = 16

outer_rate = 0.7
outer_momentum = 0.9

AXES = ("y", "zh", "core", "zl", "x")
SIZES = (4, 2, 2, 4, 4)
PLACES = list(itertools.product(*(range(n) for n in SIZES)))
NUMBER = {place: i for i, place in enumerate(PLACES)}
LENGTH = {"x": 4, "y": 4, "z": 8}
VMEM = 12 * 2**20
bf16 = jnp.bfloat16
f32 = jnp.float32


def moved(block, axis, step):
    route = []
    for y, zh, core, zl, x in PLACES:
        z = zh * 4 + zl
        if axis == "x":
            x2, y2, z2 = (x + step) % 4, y, z
        elif axis == "y":
            x2, y2, z2 = x, (y + step) % 4, z
        else:
            x2, y2, z2 = x, y, (z + step) % 8
        route.append((NUMBER[(y, zh, core, zl, x)], NUMBER[(y2, z2 // 4, core, z2 % 4, x2)]))
    return lax.ppermute(block, AXES, route)


def core_swap(block):
    return lax.ppermute(block, "core", [(0, 1), (1, 0)])


def pick(array, index):
    return lax.dynamic_index_in_dim(array, index, 0, keepdims=False)


def together(*arrays):
    return lax.optimization_barrier(tuple(arrays))


def place(blocks, index, positions, parts, out_shapes):
    count = len(blocks)

    def kernel(index_ref, *refs):
        ins, outs = refs[:count], refs[count:]
        for j in range(count):
            at = index_ref[positions[j]]
            for o, source, target in parts[j]:
                outs[o][target(at)] = ins[j][source]

    vmem = pl.BlockSpec(memory_space=pltpu.VMEM)
    return pl.pallas_call(
        kernel,
        in_specs=[pl.BlockSpec(memory_space=pltpu.SMEM)] + [vmem] * count,
        out_specs=[vmem] * len(out_shapes),
        out_shape=[jax.ShapeDtypeStruct(s, bf16) for s in out_shapes],
        compiler_params=pltpu.CompilerParams(vmem_limit_bytes=VMEM),
    )(index, *blocks)


def span(start, size, unit):
    return pl.ds(pl.multiple_of(start, unit), size)


EVERY = slice(None)


def place_first(z_blocks, x_blocks, index):
    parts = [
        [
            (
                o,
                (EVERY, slice(o * 128, o * 128 + 128)),
                lambda at: (span((at // 4) * 192, 192, 32), span((at % 4) * 128, 128, 128)),
            )
            for o in range(2)
        ]
    ] * 8
    parts += [[(2, (EVERY, EVERY), lambda at: (span(at * 48, 48, 16), EVERY))]] * 4
    positions = [*range(8), *range(12, 16)]
    return place(
        [*z_blocks, *x_blocks], index, positions, parts, [(384, 512), (384, 512), (192, 2048)]
    )


def around(index):
    return [index, (index + 3) % 4, (index + 1) % 4, (index + 2) % 4]


def place_middle(rows_blocks, columns_blocks, index):
    parts = [[(0, (EVERY, EVERY), lambda at: (span(at * 384, 384, 32), EVERY))]] * 4
    parts += [[(1, (EVERY, EVERY), lambda at: (EVERY, span(at * 512, 512, 128)))]] * 4
    return place(
        [*rows_blocks, *columns_blocks], index, range(8, 16), parts, [(1536, 512), (384, 2048)]
    )


def order_tokens(own, other, index):
    def kernel(index_ref, own_ref, other_ref, *outs):
        for k, ref in enumerate((own_ref, other_ref)):
            rows = slice(k * 256, k * 256 + 256)
            for zl in range(4):
                for j in range(4):
                    start = (zl * 4 + index_ref[12 + j]) * 256
                    outs[j][rows, zl * 128 : zl * 128 + 128] = ref[:, span(start, 128, 128)]
                    start = (zl * 4 + j) * 256 + 128
                    to = (j * 4 + zl) * 128
                    outs[4][rows, to : to + 128] = ref[:, start : start + 128]

    vmem = pl.BlockSpec(memory_space=pltpu.VMEM)
    return pl.pallas_call(
        kernel,
        in_specs=[pl.BlockSpec(memory_space=pltpu.SMEM)] + [vmem] * 2,
        out_specs=[vmem] * 5,
        out_shape=[jax.ShapeDtypeStruct(s, bf16) for s in [(512, 512)] * 4 + [(512, 2048)]],
        compiler_params=pltpu.CompilerParams(vmem_limit_bytes=VMEM),
    )(index, own, other)


def swiglu(y, gates, ups, by_step):
    scale = 1.0 / math.sqrt(D)

    def kernel(y_ref, gates_ref, ups_ref, *refs):
        blocks, out_ref = refs[:4], refs[4]

        def write(here):
            for k in range(2):
                cut = slice(k * 384, k * 384 + 384)
                gate = (gates_ref[:, cut] + blocks[(k - here) % 4][...]) * scale
                up = (ups_ref[:, cut] + blocks[(k + 2 - here) % 4][...]) * scale
                out_ref[:, cut] = (jax.nn.silu(gate) * up).astype(bf16)

        for here in range(4):
            pl.when(y_ref[0] == here)(lambda here=here: write(here))

    vmem = pl.BlockSpec(memory_space=pltpu.VMEM)
    return pl.pallas_call(
        kernel,
        in_specs=[pl.BlockSpec(memory_space=pltpu.SMEM)] + [vmem] * 6,
        out_specs=vmem,
        out_shape=jax.ShapeDtypeStruct((512, F), bf16),
        compiler_params=pltpu.CompilerParams(vmem_limit_bytes=VMEM),
    )(y.astype(jnp.int32).reshape(1), gates, ups, *by_step)


def outer_update(delta, master, moment):
    moment_new = outer_momentum * moment + delta
    master_new = master - outer_rate * (delta + outer_momentum * moment_new)
    return master_new, moment_new


def finish(hidden, weights, zh, back, gain_own, gain_other, mixed=None):
    scale = 1.0 / math.sqrt(F)

    def kernel(hidden_ref, weights_ref, back_ref, gain_own_ref, gain_other_ref, *refs):
        out = jnp.dot(hidden_ref[...], weights_ref[...], preferred_element_type=f32) * scale
        out = gain_own_ref[...] * out.astype(bf16).astype(f32)
        out = out + gain_other_ref[...] * back_ref[...].astype(f32)
        refs[-1][...] = out.astype(bf16)

    gain = pl.BlockSpec((256, 1), lambda i: (0, 0))
    more = [] if mixed is None else [mixed]
    return pl.pallas_call(
        kernel,
        grid=(4,),
        in_specs=[
            pl.BlockSpec((256, F), lambda i: (0, 0)),
            pl.BlockSpec((F, 512), lambda i: (zh, i)),
            pl.BlockSpec((256, 512), lambda i: (0, i)),
            gain,
            gain,
        ]
        + [pl.BlockSpec(memory_space=pl.ANY)] * len(more),
        out_specs=pl.BlockSpec((256, 512), lambda i: (0, 2 * i + zh)),
        out_shape=jax.ShapeDtypeStruct((256, 4096), bf16),
        input_output_aliases={5: 0} if more else {},
        compiler_params=pltpu.CompilerParams(vmem_limit_bytes=VMEM),
    )(hidden, weights, back, gain_own, gain_other, *more)


def nt_dot(rows, columns):
    return lax.dot_general(rows, columns, (((1,), (1,)), ((), ())), preferred_element_type=f32)


def body(
    pseudo_in,
    pseudo_out,
    master_in,
    master_out,
    moment_in,
    moment_out,
    tokens,
    route_ids,
    route_weights,
    counts,
):
    core = lax.axis_index("core")
    x = lax.axis_index("x")
    y = lax.axis_index("y")
    zh = lax.axis_index("zh")
    z = zh * 4 + lax.axis_index("zl")
    first_core = core == 0

    own_rows = tokens[0, 0]

    expert_ids = route_ids[0, 0]
    gate_gains = route_weights[0, 0]
    valid_rows = (jnp.arange(256, dtype=jnp.int32) < counts[0, 0]).astype(f32)
    gain_own = valid_rows * jnp.sum(gate_gains * (expert_ids == core).astype(f32), axis=1)
    gain_other = valid_rows * jnp.sum(gate_gains * (expert_ids != core).astype(f32), axis=1)

    def rows_of(a_in, a_out):
        return jnp.concatenate([a_in.transpose(0, 2, 1), a_out], axis=1)

    states = jnp.stack([rows_of(master_in, master_out), rows_of(moment_in, moment_out)], axis=1)

    grads_in = pseudo_in[0].astype(bf16).transpose(0, 2, 1).reshape(2, 8, 192, 256)
    grads_out = (
        pseudo_out[0].astype(bf16).reshape(2, 48, 8, 2, 256).transpose(0, 2, 3, 1, 4).reshape(2, 8, 96, 256)
    )
    grads = jnp.concatenate([grads_in, grads_out], axis=2)
    got = core_swap(pick(grads, 1 - core))
    total = (pick(grads, core).astype(f32) + got.astype(f32)).reshape(4, 2, 288, 256)
    low = total.astype(bf16)
    index = jnp.stack(
        [(z + k) % 8 for k in (0, 7, 6, 5, 1, 2, 3, 4)] + around(y) + around(x)
    ).astype(jnp.int32)
    *sends, kept, token_rows, states, index = together(
        *[pick(low, (y + k) % 4) for k in (1, 3, 2)], pick(total, y), own_rows, states, index
    )
    *got, other_rows, state_got, index, gain_own, gain_other = together(
        *[moved(s, "y", k) for s, k in zip(sends, (1, 3, 2))],
        core_swap(token_rows),
        core_swap(pick(states, 1 - core)),
        index,
        gain_own[:, None],
        gain_other[:, None],
    )
    for g in got:
        kept = kept + g.astype(f32)
    state_own = pick(states, core)
    send, kept, state_own, state_got = together(
        pick(kept, 1 - zh).astype(bf16), pick(kept, zh), state_own, state_got
    )
    state = jnp.where(
        first_core, jnp.stack([state_own, state_got], 1), jnp.stack([state_got, state_own], 1)
    )
    got, state = together(moved(send, "z", 4), state)
    delta = (kept + got.astype(f32)) / REPLICAS
    new_master_a, new_moment_a = outer_update(
        delta[:192].reshape(2, 96, 256), state[0, :, :96], state[1, :, :96]
    )
    new_master_b, new_moment_b = outer_update(
        delta[192:].reshape(2, 48, 256), state[0, :, 96:], state[1, :, 96:]
    )

    w_in = new_master_a.astype(bf16).reshape(192, 256)
    w_out = new_master_b.astype(bf16).reshape(96, 256)
    w_in, w_out, token_rows, other_rows = together(w_in, w_out, token_rows, other_rows)
    rows = order_tokens(token_rows, other_rows, index)
    b_1, f_1, f_4, *rest = together(
        moved(w_in, "z", 1),
        moved(w_in, "z", -1),
        moved(w_in, "z", 4),
        *[moved(w_out, "y", k) for k in (1, -1, 2)],
        *rows,
    )
    o, rows = rest[:3], rest[3:]
    parts = [
        [
            (0, (slice(c * 48, c * 48 + 48), EVERY), lambda at, c=c: (EVERY, span(at * 512 + c * 256, 256, 128)))
            for c in range(2)
        ]
    ] * 4
    p2 = place([w_out, *o], index, range(8, 12), parts, [(48, 2048)])[0]
    b_1, f_1, f_4, p2 = together(b_1, f_1, f_4, p2)
    b_2, f_3, f_2, b_3, *o = together(
        moved(b_1, "z", 1),
        moved(f_4, "z", 1),
        moved(f_1, "z", -1),
        moved(f_4, "z", -1),
        *[moved(p2, "x", k) for k in (1, -1, 2)],
    )
    p0, p1, p2 = place_first([w_in, b_1, b_2, b_3, f_1, f_2, f_3, f_4], [p2, *o], index)
    p0, p1, p2 = together(p0, p1, p2)
    weights_out = lax.all_gather(p2, ("zh", "zl"), tiled=True)

    o = together(*[moved(p0, "y", k) for k in (1, -1, 2)], *[moved(p1, "x", k) for k in (1, -1, 2)])
    p0, p1 = place_middle([p0, *o[:3]], [p1, *o[3:]], index)
    p0, p1, new_master_a, new_moment_a, new_master_b, new_moment_b = together(
        p0, p1, new_master_a, new_moment_a, new_master_b, new_moment_b
    )
    rows_here, rows_before, rows_after, rows_across, rows_1 = rows

    updated = jnp.stack(
        [
            jnp.concatenate([new_master_a, new_master_b], axis=1),
            jnp.concatenate([new_moment_a, new_moment_b], axis=1),
        ],
        axis=1,
    )
    mine = pick(updated, core)
    x_l, x_r, y_l, y_r, mine, got, total, here = together(
        moved(p0, "x", 1),
        moved(p0, "x", -1),
        moved(p1, "y", 1),
        moved(p1, "y", -1),
        mine,
        core_swap(pick(updated, 1 - core)),
        nt_dot(rows_here, p0),
        nt_dot(rows_1, p1),
    )
    final = jnp.where(first_core, jnp.stack([mine, got], 1), jnp.stack([got, mine], 1))
    new_in, new_out = final[:, :, :96].transpose(0, 1, 3, 2), final[:, :, 96:]
    (total,) = together(total + nt_dot(rows_before, x_l))
    total = total + nt_dot(rows_after, x_r)
    x_o, x_o2, y_o, y_o2, total, before, after, new_in, new_out = together(
        moved(x_l[:768], "x", 1),
        moved(x_r[768:], "x", -1),
        moved(y_l[:192], "y", 1),
        moved(y_r[192:], "y", -1),
        total,
        nt_dot(rows_1, y_l),
        nt_dot(rows_1, y_r),
        new_in,
        new_out,
    )
    halves = [total[:, :F] + nt_dot(rows_across, x_o), total[:, F:] + nt_dot(rows_across, x_o2)]
    across = jnp.concatenate([nt_dot(rows_1, y_o), nt_dot(rows_1, y_o2)], axis=1)
    hidden = swiglu(y, *halves, [here, after, across, before])

    scale_out = 1.0 / math.sqrt(F)
    back = []
    for k in range(2):
        out = jnp.dot(hidden[256:], weights_out[k * F : k * F + F], preferred_element_type=f32)
        back.append(core_swap((out * scale_out).astype(bf16)))
    mixed = finish(hidden, weights_out, 0, back[0], gain_own, gain_other)
    mixed = finish(hidden, weights_out, 1, back[1], gain_own, gain_other, mixed)

    return new_in[0], new_out[0], new_in[1], new_out[1], mixed[None, None]


def solution(mesh):
    fine = Mesh(mesh.devices.reshape(SIZES), AXES)
    replica, shard = ("y", "zh", "core"), ("zl", "x")
    state = P(None, shard, replica)
    in_specs = (
        P(replica, None, shard, None),
        P(replica, None, shard, None),
        state,
        state,
        state,
        state,
        P(replica, shard, None, None),
        P(replica, shard, None, None),
        P(replica, shard, None, None),
        P(replica, shard),
    )
    out_specs = (state, state, state, state, P(replica, shard, None, None))
    return jax.shard_map(body, mesh=fine, in_specs=in_specs, out_specs=out_specs, check_vma=False)
```

```python
import itertools
import math

import jax
import jax.numpy as jnp
from jax import lax
from jax.experimental import pallas as pl
from jax.experimental.pallas import tpu as pltpu
from jax.sharding import Mesh
from jax.sharding import PartitionSpec as P

D = 4096
F = 768
REPLICAS = 16

outer_rate = 0.7
outer_momentum = 0.9

AXES = ("y", "zh", "core", "zl", "x")
SIZES = (4, 2, 2, 4, 4)
PLACES = list(itertools.product(*(range(n) for n in SIZES)))
NUMBER = {place: i for i, place in enumerate(PLACES)}
LENGTH = {"x": 4, "y": 4, "z": 8}
VMEM = 12 * 2**20
bf16 = jnp.bfloat16
f32 = jnp.float32


def moved(block, axis, step):
    route = []
    for y, zh, core, zl, x in PLACES:
        z = zh * 4 + zl
        if axis == "x":
            x2, y2, z2 = (x + step) % 4, y, z
        elif axis == "y":
            x2, y2, z2 = x, (y + step) % 4, z
        else:
            x2, y2, z2 = x, y, (z + step) % 8
        route.append((NUMBER[(y, zh, core, zl, x)], NUMBER[(y2, z2 // 4, core, z2 % 4, x2)]))
    return lax.ppermute(block, AXES, route)


def core_swap(block):
    return lax.ppermute(block, "core", [(0, 1), (1, 0)])


def pick(array, index):
    return lax.dynamic_index_in_dim(array, index, 0, keepdims=False)


def together(*arrays):
    return lax.optimization_barrier(tuple(arrays))


def place(blocks, index, positions, parts, out_shapes):
    count = len(blocks)

    def kernel(index_ref, *refs):
        ins, outs = refs[:count], refs[count:]
        for j in range(count):
            at = index_ref[positions[j]]
            for o, source, target in parts[j]:
                outs[o][target(at)] = ins[j][source]

    vmem = pl.BlockSpec(memory_space=pltpu.VMEM)
    return pl.pallas_call(
        kernel,
        in_specs=[pl.BlockSpec(memory_space=pltpu.SMEM)] + [vmem] * count,
        out_specs=[vmem] * len(out_shapes),
        out_shape=[jax.ShapeDtypeStruct(s, bf16) for s in out_shapes],
        compiler_params=pltpu.CompilerParams(vmem_limit_bytes=VMEM),
    )(index, *blocks)


def span(start, size, unit):
    return pl.ds(pl.multiple_of(start, unit), size)


EVERY = slice(None)


def place_first(z_blocks, x_blocks, index):
    parts = [
        [
            (
                o,
                (EVERY, slice(o * 128, o * 128 + 128)),
                lambda at: (span((at // 4) * 192, 192, 32), span((at % 4) * 128, 128, 128)),
            )
            for o in range(2)
        ]
    ] * 8
    parts += [[(2, (EVERY, EVERY), lambda at: (span(at * 48, 48, 16), EVERY))]] * 4
    positions = [*range(8), *range(12, 16)]
    return place(
        [*z_blocks, *x_blocks], index, positions, parts, [(384, 512), (384, 512), (192, 2048)]
    )


def around(index):
    return [index, (index + 3) % 4, (index + 1) % 4, (index + 2) % 4]


def place_middle(rows_blocks, columns_blocks, index):
    parts = [[(0, (EVERY, EVERY), lambda at: (span(at * 384, 384, 32), EVERY))]] * 4
    parts += [[(1, (EVERY, EVERY), lambda at: (EVERY, span(at * 512, 512, 128)))]] * 4
    return place(
        [*rows_blocks, *columns_blocks], index, range(8, 16), parts, [(1536, 512), (384, 2048)]
    )


def order_tokens(own, other, index):
    def kernel(index_ref, own_ref, other_ref, *outs):
        for k, ref in enumerate((own_ref, other_ref)):

            @pl.loop(0, 8)
            def _(r, k=k, ref=ref):
                source, rows = span(r * 32, 32, 32), span(k * 256 + r * 32, 32, 32)
                for zl in range(4):
                    for j in range(4):
                        start = (zl * 4 + index_ref[12 + j]) * 256
                        outs[j][rows, zl * 128 : zl * 128 + 128] = ref[source, span(start, 128, 128)]
                        start = (zl * 4 + j) * 256 + 128
                        to = (j * 4 + zl) * 128
                        outs[4][rows, to : to + 128] = ref[source, start : start + 128]

    vmem = pl.BlockSpec(memory_space=pltpu.VMEM)
    return pl.pallas_call(
        kernel,
        in_specs=[pl.BlockSpec(memory_space=pltpu.SMEM)] + [vmem] * 2,
        out_specs=[vmem] * 5,
        out_shape=[jax.ShapeDtypeStruct(s, bf16) for s in [(512, 512)] * 4 + [(512, 2048)]],
        compiler_params=pltpu.CompilerParams(vmem_limit_bytes=VMEM),
    )(index, own, other)


def swiglu(y, gates, ups, by_step):
    scale = 1.0 / math.sqrt(D)

    def kernel(y_ref, gates_ref, ups_ref, *refs):
        blocks, out_ref = refs[:4], refs[4]

        def write(here):
            @pl.loop(0, 16)
            def _(r):
                rows = span(r * 32, 32, 32)
                for k in range(2):
                    cut = slice(k * 384, k * 384 + 384)
                    gate = (gates_ref[rows, cut] + blocks[(k - here) % 4][rows, :]) * scale
                    up = (ups_ref[rows, cut] + blocks[(k + 2 - here) % 4][rows, :]) * scale
                    out_ref[rows, cut] = (jax.nn.silu(gate) * up).astype(bf16)

        for here in range(4):
            pl.when(y_ref[0] == here)(lambda here=here: write(here))

    vmem = pl.BlockSpec(memory_space=pltpu.VMEM)
    return pl.pallas_call(
        kernel,
        in_specs=[pl.BlockSpec(memory_space=pltpu.SMEM)] + [vmem] * 6,
        out_specs=vmem,
        out_shape=jax.ShapeDtypeStruct((512, F), bf16),
        compiler_params=pltpu.CompilerParams(vmem_limit_bytes=VMEM),
    )(y.astype(jnp.int32).reshape(1), gates, ups, *by_step)


def outer_update(delta, master, moment):
    moment_new = outer_momentum * moment + delta
    master_new = master - outer_rate * (delta + outer_momentum * moment_new)
    return master_new, moment_new


def finish(hidden, weights, zh, back, gain_own, gain_other, mixed=None):
    scale = 1.0 / math.sqrt(F)

    def kernel(hidden_ref, weights_ref, back_ref, gain_own_ref, gain_other_ref, *refs):
        out = jnp.dot(hidden_ref[...], weights_ref[...], preferred_element_type=f32) * scale
        out = gain_own_ref[...] * out.astype(bf16).astype(f32)
        out = out + gain_other_ref[...] * back_ref[...].astype(f32)
        refs[-1][...] = out.astype(bf16)

    gain = pl.BlockSpec((256, 1), lambda i: (0, 0))
    more = [] if mixed is None else [mixed]
    return pl.pallas_call(
        kernel,
        grid=(4,),
        in_specs=[
            pl.BlockSpec((256, F), lambda i: (0, 0)),
            pl.BlockSpec((F, 512), lambda i: (zh, i)),
            pl.BlockSpec((256, 512), lambda i: (0, i)),
            gain,
            gain,
        ]
        + [pl.BlockSpec(memory_space=pl.ANY)] * len(more),
        out_specs=pl.BlockSpec((256, 512), lambda i: (0, 2 * i + zh)),
        out_shape=jax.ShapeDtypeStruct((256, 4096), bf16),
        input_output_aliases={5: 0} if more else {},
        compiler_params=pltpu.CompilerParams(vmem_limit_bytes=VMEM),
    )(hidden, weights, back, gain_own, gain_other, *more)


def nt_dot(rows, columns):
    return lax.dot_general(rows, columns, (((1,), (1,)), ((), ())), preferred_element_type=f32)


def body(
    pseudo_in,
    pseudo_out,
    master_in,
    master_out,
    moment_in,
    moment_out,
    tokens,
    route_ids,
    route_weights,
    counts,
):
    core = lax.axis_index("core")
    x = lax.axis_index("x")
    y = lax.axis_index("y")
    zh = lax.axis_index("zh")
    z = zh * 4 + lax.axis_index("zl")
    first_core = core == 0

    own_rows = tokens[0, 0]

    expert_ids = route_ids[0, 0]
    gate_gains = route_weights[0, 0]
    valid_rows = (jnp.arange(256, dtype=jnp.int32) < counts[0, 0]).astype(f32)
    gain_own = valid_rows * jnp.sum(gate_gains * (expert_ids == core).astype(f32), axis=1)
    gain_other = valid_rows * jnp.sum(gate_gains * (expert_ids != core).astype(f32), axis=1)

    def rows_of(a_in, a_out):
        return jnp.concatenate([a_in.transpose(0, 2, 1), a_out], axis=1)

    states = jnp.stack([rows_of(master_in, master_out), rows_of(moment_in, moment_out)], axis=1)

    grads_in = pseudo_in[0].astype(bf16).transpose(0, 2, 1).reshape(2, 8, 192, 256)
    grads_out = (
        pseudo_out[0].astype(bf16).reshape(2, 48, 8, 2, 256).transpose(0, 2, 3, 1, 4).reshape(2, 8, 96, 256)
    )
    grads = jnp.concatenate([grads_in, grads_out], axis=2)
    got = core_swap(pick(grads, 1 - core))
    total = (pick(grads, core).astype(f32) + got.astype(f32)).reshape(4, 2, 288, 256)
    low = total.astype(bf16)
    index = jnp.stack(
        [(z + k) % 8 for k in (0, 7, 6, 5, 1, 2, 3, 4)] + around(y) + around(x)
    ).astype(jnp.int32)
    *sends, kept, token_rows, states, index = together(
        *[pick(low, (y + k) % 4) for k in (1, 3, 2)], pick(total, y), own_rows, states, index
    )
    *got, other_rows, state_got, index, gain_own, gain_other = together(
        *[moved(s, "y", k) for s, k in zip(sends, (1, 3, 2))],
        core_swap(token_rows),
        core_swap(pick(states, 1 - core)),
        index,
        gain_own[:, None],
        gain_other[:, None],
    )
    for g in got:
        kept = kept + g.astype(f32)
    state_own = pick(states, core)
    send, kept, state_own, state_got = together(
        pick(kept, 1 - zh).astype(bf16), pick(kept, zh), state_own, state_got
    )
    state = jnp.where(
        first_core, jnp.stack([state_own, state_got], 1), jnp.stack([state_got, state_own], 1)
    )
    got, state = together(moved(send, "z", 4), state)
    delta = (kept + got.astype(f32)) / REPLICAS
    new_master_a, new_moment_a = outer_update(
        delta[:192].reshape(2, 96, 256), state[0, :, :96], state[1, :, :96]
    )
    new_master_b, new_moment_b = outer_update(
        delta[192:].reshape(2, 48, 256), state[0, :, 96:], state[1, :, 96:]
    )

    w_in = new_master_a.astype(bf16).reshape(192, 256)
    w_out = new_master_b.astype(bf16).reshape(96, 256)
    w_in, w_out = together(w_in, w_out)
    b_1, f_1, f_4, *o = together(
        moved(w_in, "z", 1),
        moved(w_in, "z", -1),
        moved(w_in, "z", 4),
        *[moved(w_out, "y", k) for k in (1, -1, 2)],
    )
    parts = [
        [
            (0, (slice(c * 48, c * 48 + 48), EVERY), lambda at, c=c: (EVERY, span(at * 512 + c * 256, 256, 128)))
            for c in range(2)
        ]
    ] * 4
    p2 = place([w_out, *o], index, range(8, 12), parts, [(48, 2048)])[0]
    b_1, f_1, f_4, p2 = together(b_1, f_1, f_4, p2)
    b_2, f_3, f_2, b_3, *o = together(
        moved(b_1, "z", 1),
        moved(f_4, "z", 1),
        moved(f_1, "z", -1),
        moved(f_4, "z", -1),
        *[moved(p2, "x", k) for k in (1, -1, 2)],
    )
    p0, p1, p2 = place_first([w_in, b_1, b_2, b_3, f_1, f_2, f_3, f_4], [p2, *o], index)
    p0, p1, p2 = together(p0, p1, p2)
    weights_out = lax.all_gather(p2, ("zh", "zl"), tiled=True)

    o = together(*[moved(p0, "y", k) for k in (1, -1, 2)], *[moved(p1, "x", k) for k in (1, -1, 2)])
    p0, p1 = place_middle([p0, *o[:3]], [p1, *o[3:]], index)
    p0, p1, new_master_a, new_moment_a, new_master_b, new_moment_b, token_rows, other_rows = together(
        p0, p1, new_master_a, new_moment_a, new_master_b, new_moment_b, token_rows, other_rows
    )
    rows_here, rows_before, rows_after, rows_across, rows_1 = order_tokens(token_rows, other_rows, index)

    updated = jnp.stack(
        [
            jnp.concatenate([new_master_a, new_master_b], axis=1),
            jnp.concatenate([new_moment_a, new_moment_b], axis=1),
        ],
        axis=1,
    )
    mine = pick(updated, core)
    x_l, x_r, y_l, y_r, mine, got, total, here = together(
        moved(p0, "x", 1),
        moved(p0, "x", -1),
        moved(p1, "y", 1),
        moved(p1, "y", -1),
        mine,
        core_swap(pick(updated, 1 - core)),
        nt_dot(rows_here, p0),
        nt_dot(rows_1, p1),
    )
    final = jnp.where(first_core, jnp.stack([mine, got], 1), jnp.stack([got, mine], 1))
    new_in, new_out = final[:, :, :96].transpose(0, 1, 3, 2), final[:, :, 96:]
    (total,) = together(total + nt_dot(rows_before, x_l))
    total = total + nt_dot(rows_after, x_r)
    x_o, x_o2, y_o, y_o2, total, before, after, new_in, new_out = together(
        moved(x_l[:768], "x", 1),
        moved(x_r[768:], "x", -1),
        moved(y_l[:192], "y", 1),
        moved(y_r[192:], "y", -1),
        total,
        nt_dot(rows_1, y_l),
        nt_dot(rows_1, y_r),
        new_in,
        new_out,
    )
    halves = [total[:, :F] + nt_dot(rows_across, x_o), total[:, F:] + nt_dot(rows_across, x_o2)]
    across = jnp.concatenate([nt_dot(rows_1, y_o), nt_dot(rows_1, y_o2)], axis=1)
    hidden = swiglu(y, *halves, [here, after, across, before])

    scale_out = 1.0 / math.sqrt(F)
    back = []
    for k in range(2):
        out = jnp.dot(hidden[256:], weights_out[k * F : k * F + F], preferred_element_type=f32)
        back.append(core_swap((out * scale_out).astype(bf16)))
    mixed = finish(hidden, weights_out, 0, back[0], gain_own, gain_other)
    mixed = finish(hidden, weights_out, 1, back[1], gain_own, gain_other, mixed)

    return new_in[0], new_out[0], new_in[1], new_out[1], mixed[None, None]


def solution(mesh):
    fine = Mesh(mesh.devices.reshape(SIZES), AXES)
    replica, shard = ("y", "zh", "core"), ("zl", "x")
    state = P(None, shard, replica)
    in_specs = (
        P(replica, None, shard, None),
        P(replica, None, shard, None),
        state,
        state,
        state,
        state,
        P(replica, shard, None, None),
        P(replica, shard, None, None),
        P(replica, shard, None, None),
        P(replica, shard),
    )
    out_specs = (state, state, state, state, P(replica, shard, None, None))
    return jax.shard_map(body, mesh=fine, in_specs=in_specs, out_specs=out_specs, check_vma=False)
```

```python
import itertools
import math

import jax
import jax.numpy as jnp
from jax import lax
from jax.experimental import pallas as pl
from jax.experimental.pallas import tpu as pltpu
from jax.sharding import Mesh
from jax.sharding import PartitionSpec as P

D = 4096
F = 768
REPLICAS = 16

outer_rate = 0.7
outer_momentum = 0.9

AXES = ("y", "zh", "core", "zl", "x")
SIZES = (4, 2, 2, 4, 4)
PLACES = list(itertools.product(*(range(n) for n in SIZES)))
NUMBER = {place: i for i, place in enumerate(PLACES)}
LENGTH = {"x": 4, "y": 4, "z": 8}
VMEM = 12 * 2**20
bf16 = jnp.bfloat16
f32 = jnp.float32


def moved(block, axis, step):
    route = []
    for y, zh, core, zl, x in PLACES:
        z = zh * 4 + zl
        if axis == "x":
            x2, y2, z2 = (x + step) % 4, y, z
        elif axis == "y":
            x2, y2, z2 = x, (y + step) % 4, z
        else:
            x2, y2, z2 = x, y, (z + step) % 8
        route.append((NUMBER[(y, zh, core, zl, x)], NUMBER[(y2, z2 // 4, core, z2 % 4, x2)]))
    return lax.ppermute(block, AXES, route)


def core_swap(block):
    return lax.ppermute(block, "core", [(0, 1), (1, 0)])


def pick(array, index):
    return lax.dynamic_index_in_dim(array, index, 0, keepdims=False)


def together(*arrays):
    return lax.optimization_barrier(tuple(arrays))


def place(blocks, index, positions, parts, out_shapes):
    count = len(blocks)

    def kernel(index_ref, *refs):
        ins, outs = refs[:count], refs[count:]
        for j in range(count):
            at = index_ref[positions[j]]
            for o, source, target in parts[j]:
                outs[o][target(at)] = ins[j][source]

    vmem = pl.BlockSpec(memory_space=pltpu.VMEM)
    return pl.pallas_call(
        kernel,
        in_specs=[pl.BlockSpec(memory_space=pltpu.SMEM)] + [vmem] * count,
        out_specs=[vmem] * len(out_shapes),
        out_shape=[jax.ShapeDtypeStruct(s, bf16) for s in out_shapes],
        compiler_params=pltpu.CompilerParams(vmem_limit_bytes=VMEM),
    )(index, *blocks)


def span(start, size, unit):
    return pl.ds(pl.multiple_of(start, unit), size)


EVERY = slice(None)


def place_first(z_blocks, x_blocks, index):
    parts = [
        [
            (
                o,
                (EVERY, slice(o * 128, o * 128 + 128)),
                lambda at: (span((at // 4) * 192, 192, 32), span((at % 4) * 128, 128, 128)),
            )
            for o in range(2)
        ]
    ] * 8
    parts += [[(2, (EVERY, EVERY), lambda at: (span(at * 48, 48, 16), EVERY))]] * 4
    positions = [*range(8), *range(12, 16)]
    return place(
        [*z_blocks, *x_blocks], index, positions, parts, [(384, 512), (384, 512), (192, 2048)]
    )


def around(index):
    return [index, (index + 3) % 4, (index + 1) % 4, (index + 2) % 4]


def place_middle(rows_blocks, columns_blocks, index):
    parts = [[(0, (EVERY, EVERY), lambda at: (span(at * 384, 384, 32), EVERY))]] * 4
    parts += [[(1, (EVERY, EVERY), lambda at: (EVERY, span(at * 512, 512, 128)))]] * 4
    return place(
        [*rows_blocks, *columns_blocks], index, range(8, 16), parts, [(1536, 512), (384, 2048)]
    )


def order_tokens(own, other, index):
    def kernel(index_ref, own_ref, other_ref, *outs):
        for k, ref in enumerate((own_ref, other_ref)):

            @pl.loop(0, 8)
            def _(r, k=k, ref=ref):
                source, rows = span(r * 32, 32, 32), span(k * 256 + r * 32, 32, 32)
                for zl in range(4):
                    for j in range(4):
                        start = (zl * 4 + index_ref[12 + j]) * 256
                        outs[j][rows, zl * 128 : zl * 128 + 128] = ref[source, span(start, 128, 128)]
                        start = (zl * 4 + j) * 256 + 128
                        to = (j * 4 + zl) * 128
                        outs[4][rows, to : to + 128] = ref[source, start : start + 128]

    vmem = pl.BlockSpec(memory_space=pltpu.VMEM)
    return pl.pallas_call(
        kernel,
        in_specs=[pl.BlockSpec(memory_space=pltpu.SMEM)] + [vmem] * 2,
        out_specs=[vmem] * 5,
        out_shape=[jax.ShapeDtypeStruct(s, bf16) for s in [(512, 512)] * 4 + [(512, 2048)]],
        compiler_params=pltpu.CompilerParams(vmem_limit_bytes=VMEM),
    )(index, own, other)


def swiglu(y, gates, ups, by_step):
    scale = 1.0 / math.sqrt(D)

    def kernel(y_ref, gates_ref, ups_ref, *refs):
        blocks, out_ref = refs[:4], refs[4]

        def write(here):
            @pl.loop(0, 16)
            def _(r):
                rows = span(r * 32, 32, 32)
                for k in range(2):
                    cut = slice(k * 384, k * 384 + 384)
                    gate = (gates_ref[rows, cut] + blocks[(k - here) % 4][rows, :]) * scale
                    up = (ups_ref[rows, cut] + blocks[(k + 2 - here) % 4][rows, :]) * scale
                    out_ref[rows, cut] = (jax.nn.silu(gate) * up).astype(bf16)

        for here in range(4):
            pl.when(y_ref[0] == here)(lambda here=here: write(here))

    vmem = pl.BlockSpec(memory_space=pltpu.VMEM)
    return pl.pallas_call(
        kernel,
        in_specs=[pl.BlockSpec(memory_space=pltpu.SMEM)] + [vmem] * 6,
        out_specs=vmem,
        out_shape=jax.ShapeDtypeStruct((512, F), bf16),
        compiler_params=pltpu.CompilerParams(vmem_limit_bytes=VMEM),
    )(y.astype(jnp.int32).reshape(1), gates, ups, *by_step)


def outer_update(delta, master, moment):
    moment_new = outer_momentum * moment + delta
    master_new = master - outer_rate * (delta + outer_momentum * moment_new)
    return master_new, moment_new


def finish(hidden, weights, zh, back, gain_own, gain_other, mixed=None):
    scale = 1.0 / math.sqrt(F)

    def kernel(hidden_ref, weights_ref, back_ref, gain_own_ref, gain_other_ref, *refs):
        out = jnp.dot(hidden_ref[...], weights_ref[...], preferred_element_type=f32) * scale
        out = gain_own_ref[...] * out.astype(bf16).astype(f32)
        out = out + gain_other_ref[...] * back_ref[...].astype(f32)
        refs[-1][...] = out.astype(bf16)

    gain = pl.BlockSpec((256, 1), lambda i: (0, 0))
    more = [] if mixed is None else [mixed]
    return pl.pallas_call(
        kernel,
        grid=(4,),
        in_specs=[
            pl.BlockSpec((256, F), lambda i: (0, 0)),
            pl.BlockSpec((F, 512), lambda i: (zh, i)),
            pl.BlockSpec((256, 512), lambda i: (0, i)),
            gain,
            gain,
        ]
        + [pl.BlockSpec(memory_space=pl.ANY)] * len(more),
        out_specs=pl.BlockSpec((256, 512), lambda i: (0, 2 * i + zh)),
        out_shape=jax.ShapeDtypeStruct((256, 4096), bf16),
        input_output_aliases={5: 0} if more else {},
        compiler_params=pltpu.CompilerParams(vmem_limit_bytes=VMEM),
    )(hidden, weights, back, gain_own, gain_other, *more)


def nt_dot(rows, columns):
    return lax.dot_general(rows, columns, (((1,), (1,)), ((), ())), preferred_element_type=f32)


def body(
    pseudo_in,
    pseudo_out,
    master_in,
    master_out,
    moment_in,
    moment_out,
    tokens,
    route_ids,
    route_weights,
    counts,
):
    core = lax.axis_index("core")
    x = lax.axis_index("x")
    y = lax.axis_index("y")
    zh = lax.axis_index("zh")
    z = zh * 4 + lax.axis_index("zl")
    first_core = core == 0

    own_rows = tokens[0, 0]

    expert_ids = route_ids[0, 0]
    gate_gains = route_weights[0, 0]
    valid_rows = (jnp.arange(256, dtype=jnp.int32) < counts[0, 0]).astype(f32)
    gain_own = valid_rows * jnp.sum(gate_gains * (expert_ids == core).astype(f32), axis=1)
    gain_other = valid_rows * jnp.sum(gate_gains * (expert_ids != core).astype(f32), axis=1)

    def rows_of(a_in, a_out):
        return jnp.concatenate([a_in.transpose(0, 2, 1), a_out], axis=1)

    states = jnp.stack([rows_of(master_in, master_out), rows_of(moment_in, moment_out)], axis=1)

    grads_in = pseudo_in[0].astype(bf16).transpose(0, 2, 1).reshape(2, 8, 192, 256)
    grads_out = (
        pseudo_out[0].astype(bf16).reshape(2, 48, 8, 2, 256).transpose(0, 2, 3, 1, 4).reshape(2, 8, 96, 256)
    )
    grads = jnp.concatenate([grads_in, grads_out], axis=2)
    got = core_swap(pick(grads, 1 - core))
    total = (pick(grads, core).astype(f32) + got.astype(f32)).reshape(4, 2, 288, 256)
    low = total.astype(bf16)
    index = jnp.stack(
        [(z + k) % 8 for k in (0, 7, 6, 5, 1, 2, 3, 4)] + around(y) + around(x)
    ).astype(jnp.int32)
    *sends, kept, token_rows, states, index = together(
        *[pick(low, (y + k) % 4) for k in (1, 3, 2)], pick(total, y), own_rows, states, index
    )
    *got, other_rows, state_got, index, gain_own, gain_other = together(
        *[moved(s, "y", k) for s, k in zip(sends, (1, 3, 2))],
        core_swap(token_rows),
        core_swap(pick(states, 1 - core)),
        index,
        gain_own[:, None],
        gain_other[:, None],
    )
    for g in got:
        kept = kept + g.astype(f32)
    state_own = pick(states, core)
    send, kept, state_own, state_got = together(
        pick(kept, 1 - zh).astype(bf16), pick(kept, zh), state_own, state_got
    )
    state = jnp.where(
        first_core, jnp.stack([state_own, state_got], 1), jnp.stack([state_got, state_own], 1)
    )
    got, state = together(moved(send, "z", 4), state)
    delta = (kept + got.astype(f32)) / REPLICAS
    new_master_a, new_moment_a = outer_update(
        delta[:192].reshape(2, 96, 256), state[0, :, :96], state[1, :, :96]
    )
    new_master_b, new_moment_b = outer_update(
        delta[192:].reshape(2, 48, 256), state[0, :, 96:], state[1, :, 96:]
    )

    w_in = new_master_a.astype(bf16).reshape(192, 256)
    w_out = new_master_b.astype(bf16).reshape(96, 256)
    w_in, w_out = together(w_in, w_out)
    f_4, b_1, f_1, *o = together(
        moved(w_in, "z", 4),
        moved(w_in, "z", 1),
        moved(w_in, "z", -1),
        *[moved(w_out, "y", k) for k in (1, -1, 2)],
    )
    parts = [
        [
            (0, (slice(c * 48, c * 48 + 48), EVERY), lambda at, c=c: (EVERY, span(at * 512 + c * 256, 256, 128)))
            for c in range(2)
        ]
    ] * 4
    p2 = place([w_out, *o], index, range(8, 12), parts, [(48, 2048)])[0]
    b_1, f_1, f_4, p2 = together(b_1, f_1, f_4, p2)
    b_2, f_3, f_2, b_3, *o = together(
        moved(b_1, "z", 1),
        moved(f_4, "z", 1),
        moved(f_1, "z", -1),
        moved(f_4, "z", -1),
        *[moved(p2, "x", k) for k in (1, -1, 2)],
    )
    p0, p1, p2 = place_first([w_in, b_1, b_2, b_3, f_1, f_2, f_3, f_4], [p2, *o], index)
    p0, p1, p2 = together(p0, p1, p2)
    weights_out = lax.all_gather(p2, ("zh", "zl"), tiled=True)

    o = together(*[f(k) for k in (2, 1, -1) for f in (lambda k: moved(p0, "y", k), lambda k: moved(p1, "x", k))])
    o = [o[2], o[4], o[0], o[3], o[5], o[1]]
    p0, p1 = place_middle([p0, *o[:3]], [p1, *o[3:]], index)
    p0, p1, new_master_a, new_moment_a, new_master_b, new_moment_b, token_rows, other_rows = together(
        p0, p1, new_master_a, new_moment_a, new_master_b, new_moment_b, token_rows, other_rows
    )
    rows_here, rows_before, rows_after, rows_across, rows_1 = order_tokens(token_rows, other_rows, index)

    updated = jnp.stack(
        [
            jnp.concatenate([new_master_a, new_master_b], axis=1),
            jnp.concatenate([new_moment_a, new_moment_b], axis=1),
        ],
        axis=1,
    )
    mine = pick(updated, core)
    x_l, x_r, y_l, y_r, mine, got, total, here = together(
        moved(p0, "x", 1),
        moved(p0, "x", -1),
        moved(p1, "y", 1),
        moved(p1, "y", -1),
        mine,
        core_swap(pick(updated, 1 - core)),
        nt_dot(rows_here, p0),
        nt_dot(rows_1, p1),
    )
    final = jnp.where(first_core, jnp.stack([mine, got], 1), jnp.stack([got, mine], 1))
    new_in, new_out = final[:, :, :96].transpose(0, 1, 3, 2), final[:, :, 96:]
    (total,) = together(total + nt_dot(rows_before, x_l))
    total = total + nt_dot(rows_after, x_r)
    x_o, x_o2, y_o, y_o2, total, before, after, new_in, new_out, weights_out = together(
        moved(x_l[:768], "x", 1),
        moved(x_r[768:], "x", -1),
        moved(y_l[:192], "y", 1),
        moved(y_r[192:], "y", -1),
        total,
        nt_dot(rows_1, y_l),
        nt_dot(rows_1, y_r),
        new_in,
        new_out,
        weights_out,
    )
    halves = [total[:, :F] + nt_dot(rows_across, x_o), total[:, F:] + nt_dot(rows_across, x_o2)]
    across = jnp.concatenate([nt_dot(rows_1, y_o), nt_dot(rows_1, y_o2)], axis=1)
    hidden = swiglu(y, *halves, [here, after, across, before])

    scale_out = 1.0 / math.sqrt(F)
    back = []
    for k in range(2):
        out = jnp.dot(hidden[256:], weights_out[k * F : k * F + F], preferred_element_type=f32)
        back.append(core_swap((out * scale_out).astype(bf16)))
    mixed = finish(hidden, weights_out, 0, back[0], gain_own, gain_other)
    mixed = finish(hidden, weights_out, 1, back[1], gain_own, gain_other, mixed)

    return new_in[0], new_out[0], new_in[1], new_out[1], mixed[None, None]


def solution(mesh):
    fine = Mesh(mesh.devices.reshape(SIZES), AXES)
    replica, shard = ("y", "zh", "core"), ("zl", "x")
    state = P(None, shard, replica)
    in_specs = (
        P(replica, None, shard, None),
        P(replica, None, shard, None),
        state,
        state,
        state,
        state,
        P(replica, shard, None, None),
        P(replica, shard, None, None),
        P(replica, shard, None, None),
        P(replica, shard),
    )
    out_specs = (state, state, state, state, P(replica, shard, None, None))
    return jax.shard_map(body, mesh=fine, in_specs=in_specs, out_specs=out_specs, check_vma=False)
```
